128 devices in a mesh: stream: 8 (over x_lo, y), cross: 16 (over z, x_hi, core).
Axes of the slice: x: 4 (x_hi: 2, x_lo: 2; x = x_hi * 2 + x_lo), y: 4, z: 4, core: 2. Of those that a mesh axis runs over, the one named last changes fastest.
Arguments:
- basis: bfloat16 [786432, 256], P(('stream', 'cross')), may hold values from -24 to 24
- volume: float32 [786432], P(('stream', 'cross')), may hold values from 0.3 to 3
- own_blocks: bfloat16 [12288, 7, 64, 128], P(('stream', 'cross')), may hold values from -0.25 to 0.25
- own_cols: int32 [12288, 7], P(('stream', 'cross')), may hold values from 0 to 95
- border_blocks: bfloat16 [128, 4, 8, 64, 128], P(('stream', 'cross')), may hold values from -0.25 to 0.25
- border_cols: int32 [128, 4, 8], P(('stream', 'cross')), may hold values from 0 to 95
- border_rows: int32 [128, 4, 8], P(('stream', 'cross')), may hold values from 0 to 95
Outputs:
- applied_basis: bfloat16 [2, 786432, 256], P(None, ('stream', 'cross'))
- reduced_operator: float32 [256, 2, 256], P(('stream', 'cross'))
The draws below stay inside these ranges and needn't reach their ends.
Inputs may be any that keep to these rules, and one draw needn't show every extreme that they name: `own_cols`: block indices within the device's own tile. `border_cols`: block indices within the sending tile. `border_rows`: block rows within the receiving neighbour's tile.
All inputs are finite; a program needn't handle non-finite values.
Results may differ from the reference program's by a relative error of at most 0.003.
Values may be sent and summed in bfloat16 or wider, within the bound.
A program may use at most 128 MiB of HBM per device.

```python
import math
import jax
import jax.numpy as jnp
from jax import lax

MODES = 256
BS = 64
KOWN = 7
BLK_DEV = 96
NBORD = 8
TILES = 128
BLOCKS = 12288
CELLS = 786432
N_STREAM = 8
N_CROSS = 16


def with_ends(values, own_key, smallest, largest):
    longest = values.shape.index(max(values.shape))
    spots = []
    for shift in (0, 1):
        where = [jax.random.randint(jax.random.fold_in(own_key, axis), (), 0, length) for axis, length in enumerate(values.shape)]
        where[longest] = (where[longest] + shift) % values.shape[longest]
        spots.append(tuple(where))
    return values.at[spots[0]].set(smallest).at[spots[1]].set(largest)


def strengthened(array, own_key, source, target, parts, factor):
    owner, partner = [(jnp.arange(array.shape[axis_at]) // (array.shape[axis_at] // parts)).reshape([-1 if axis == axis_at else 1 for axis in range(array.ndim)]) for axis_at in (source, target)]
    chosen = jax.random.permutation(own_key, parts)[partner]
    strong = (owner == chosen) | (owner == (partner + parts // 2) % parts)
    return jnp.where(strong, factor * array, array)


def block_levels(key, extent, pieces, smallest, largest):
    factor_of = 1.0
    for dim, shards_of in pieces:
        draws = jax.random.uniform(jax.random.fold_in(jax.random.fold_in(key, 6), dim), (shards_of,), jnp.float32, smallest / len(pieces), largest / len(pieces))
        factor_of = factor_of * jnp.repeat(jnp.exp(draws), extent[dim] // shards_of).reshape((-1,) + (1,) * (len(extent) - 1 - dim))
    return factor_of


def normal_values(key, dims, deviation, reach, pieces=(), kind=jnp.bfloat16):
    values = deviation * jax.random.normal(key, dims, jnp.float32)
    if pieces:
        values = values * block_levels(key, dims, pieces, -0.22, 0.18)
    return jnp.clip(values, -reach, reach).astype(kind)


def noise_with(key, dims, deviation, most, cuts, heavy, kind=jnp.bfloat16):
    values = deviation * jax.random.normal(key, dims, jnp.float32)
    if cuts:
        values = values * block_levels(key, dims, cuts, -0.22, 0.18)
    return jnp.clip(strengthened(values, jax.random.fold_in(key, 3), *heavy), -most, most).astype(kind)


def setup_inputs(seed: int = 0) -> dict:
    seeds = jax.random.split(jax.random.key(seed), 8)
    basis = noise_with(seeds[0], (CELLS, MODES), 1.0, 24.0, ((0, 128),), (0, 1, 128, 5.5))
    volume = jnp.clip(jnp.exp(math.log(3.0) - 2.3025851 * jax.random.uniform(seeds[1], (CELLS,), jnp.float32) ** block_levels(seeds[1], (CELLS,), ((0, 128),), -0.2, 0.2)), 0.3, 3.0)
    own_blocks = normal_values(seeds[2], (BLOCKS, KOWN, BS, 2 * BS), (BS * KOWN) ** -0.5, 0.25, ((0, 128),))
    own_cols = with_ends(jax.random.randint(seeds[3], (BLOCKS, KOWN), 0, BLK_DEV), jax.random.fold_in(seeds[3], 1), 0, BLK_DEV - 1).astype(jnp.int32)
    border_blocks = normal_values(seeds[4], (TILES, 4, NBORD, BS, 2 * BS), (BS * KOWN) ** -0.5, 0.25, ((0, 128),))
    border_cols = with_ends(jax.random.randint(seeds[5], (TILES, 4, NBORD), 0, BLK_DEV), jax.random.fold_in(seeds[5], 1), 0, BLK_DEV - 1).astype(jnp.int32)
    border_rows = with_ends(jax.random.randint(seeds[6], (TILES, 4, NBORD), 0, BLK_DEV), jax.random.fold_in(seeds[6], 1), 0, BLK_DEV - 1).astype(jnp.int32)
    return {"basis": basis, "volume": volume, "own_blocks": own_blocks, "own_cols": own_cols, "border_blocks": border_blocks, "border_cols": border_cols, "border_rows": border_rows}


def move_tiles(values, axis, forward):
    count = values.shape[axis]
    lead = jnp.zeros_like(lax.slice_in_dim(values, 0, 1, axis=axis))
    if forward:
        return jnp.concatenate([lead, lax.slice_in_dim(values, 0, count - 1, axis=axis)], axis=axis)
    return jnp.concatenate([lax.slice_in_dim(values, 1, count, axis=axis), lead], axis=axis)

def reference(basis, volume, own_blocks, own_cols, border_blocks, border_cols, border_rows):
    tile_count = N_STREAM * N_CROSS
    basis_tiles = basis.reshape(tile_count, BLK_DEV, BS, MODES)
    block_tiles = own_blocks.reshape(tile_count, BLK_DEV, KOWN, BS, 2 * BS)
    column_tiles = own_cols.reshape(tile_count, BLK_DEV, KOWN)
    volume_tiles = volume.reshape(tile_count, BLK_DEV, 1, BS, 1)
    norm_factor = 1.0 / math.sqrt(CELLS)

    def border_terms(packed):
        blocks, columns, basis_tile = packed
        sources = basis_tile[columns]
        return jnp.einsum('dncr,dncm->dnrm', blocks.astype(jnp.float32), sources.astype(jnp.float32))
    partial_rows = lax.map(border_terms, (border_blocks, border_cols, basis_tiles))
    grid_rows = partial_rows.reshape(N_STREAM, N_CROSS, 4, NBORD, 2 * BS, MODES)
    grid_targets = border_rows.reshape(N_STREAM, N_CROSS, 4, NBORD)
    incoming = jnp.stack([move_tiles(grid_rows[:, :, 0], 0, True), move_tiles(grid_rows[:, :, 1], 0, False), move_tiles(grid_rows[:, :, 2], 1, True), move_tiles(grid_rows[:, :, 3], 1, False)], axis=2)
    incoming = incoming.reshape(tile_count, 4 * NBORD, 2 * BS, MODES)
    targets = jnp.stack([move_tiles(grid_targets[:, :, 0], 0, True), move_tiles(grid_targets[:, :, 1], 0, False), move_tiles(grid_targets[:, :, 2], 1, True), move_tiles(grid_targets[:, :, 3], 1, False)], axis=2)
    targets = targets.reshape(tile_count, 4 * NBORD).astype(jnp.int32)

    def one_tile(total, packed):
        blocks, columns, basis_tile, cell_volume, rows_in, target_rows = packed
        gathered = basis_tile[columns]
        applied = jnp.einsum('bkcr,bkcm->brm', blocks.astype(jnp.float32), gathered.astype(jnp.float32))
        applied = applied.at[target_rows].add(rows_in)
        split = applied.reshape(BLK_DEV, 2, BS, MODES)
        weighted = (split * cell_volume * norm_factor).astype(jnp.bfloat16)
        term = jnp.einsum('bca,btcm->atm', basis_tile.astype(jnp.float32), weighted.astype(jnp.float32), precision=lax.Precision.HIGHEST)
        return (total + term, split.astype(jnp.bfloat16))
    start = jnp.zeros((MODES, 2, MODES), jnp.float32)
    reduced, outputs = lax.scan(one_tile, start, (block_tiles, column_tiles, basis_tiles, volume_tiles, incoming, targets))
    applied_basis = outputs.transpose(2, 0, 1, 3, 4).reshape(2, CELLS, MODES)
    return (applied_basis, reduced)
```

```python
import functools
import math

import jax
import jax.numpy as jnp
from jax import lax
from jax.experimental import pallas as pl
from jax.experimental.pallas import tpu as pltpu
from jax.sharding import PartitionSpec as P

MESH = pl.DeviceIdType.MESH
F32, BF16, I32 = jnp.float32, jnp.bfloat16, jnp.int32

ROWS = 96
KOWN = 7
BS = 64
MODES = 256
NB = 8
SLOTS = 4 * NB
UNROLL = 16
STEPS = ROWS // UNROLL
PROJ = 8

CONTRACT_FIRST = (((0,), (0,)), ((), ()))


def place():
    s = lax.axis_index("stream")
    c = lax.axis_index("cross")
    return (s // 4, s % 4, c // 4, (c // 2) % 2), c % 2


def ident(chip, core):
    return (chip[0] * 4 + chip[1], chip[2] * 4 + chip[3] * 2 + core)


def kernel(
    norm,
    own_cols, border_cols, border_rows,
    basis_h, volume, own_h, border_h,
    applied_out, reduced_out,
    own, basis, sums, volb, send_rows, send_b, recv_rows, recv_a, recv_b, table_v, table,
    w_chunk, w_slot, part, q, pair, h, recv_yz, recv_x,
    own_sem, basis_sem, table_sem, rows_ss, rows_rs, a_ss, a_rs, b_ss, b_rs, pair_sem, yz_sem, x_sem,
):
    s, c = lax.axis_index("stream"), lax.axis_index("cross")
    chip, core = place()
    xl, y, z, xh = chip
    mate = ident(chip, 1 - core)

    def yz_peer(k):
        return (xl, (y + k // 4) % 4, (z + k % 4) % 4, xh)

    def x_peer(k):
        return ((xl + k // 2) % 2, y, z, (xh + k % 2) % 2)

    sides = [
        (s < 7, (s + 1, c), s > 0),
        (s > 0, (s - 1, c), s < 7),
        (c < 15, (s, c + 1), c > 0),
        (c > 0, (s, c - 1), c < 15),
    ]

    basis_copy = pltpu.make_async_copy(basis_h, basis, basis_sem)
    basis_copy.start()

    def own_copy(step):
        rows = pl.ds(step * UNROLL, UNROLL)
        return pltpu.make_async_copy(own_h.at[rows], own.at[rows], own_sem.at[step])

    barrier = pltpu.get_barrier_semaphore()
    for may_send, target, _ in sides:
        @pl.when(may_send)
        def _():
            pl.semaphore_signal(barrier, inc=1, device_id=target, device_id_type=MESH)
    pl.semaphore_signal(barrier, inc=1, device_id=mate, device_id_type=MESH)

    @pl.loop(1, 16)
    def _(k):
        pl.semaphore_signal(barrier, inc=1, device_id=ident(yz_peer(k), core), device_id_type=MESH)

    for k in range(1, 4):
        pl.semaphore_signal(barrier, inc=1, device_id=ident(x_peer(k), core), device_id_type=MESH)

    for step in range(STEPS):
        own_copy(step).start()

    for d in range(4):
        for n in range(NB):
            send_rows[d, pl.ds(n, 1), :] = jnp.full((1, 128), border_rows[d, n], I32)
    for d, (_, _, may_receive) in enumerate(sides):
        @pl.when(jnp.logical_not(may_receive))
        def _():
            recv_rows[d] = jnp.zeros((NB, 128), I32)
            recv_a[d] = jnp.zeros((NB, BS, 2 * BS), BF16)
            recv_b[d] = jnp.zeros((NB, BS, MODES), BF16)

    basis_copy.wait()
    for d in range(4):
        for n in range(NB):
            send_b[d, n] = basis[border_cols[d, n]]

    greeted = sum(jnp.where(may_receive, 1, 0) for _, _, may_receive in sides)
    pl.semaphore_wait(barrier, greeted + 19)

    def border_copy(d, which):
        source, landing, sent, received = (
            (send_rows, recv_rows, rows_ss, rows_rs),
            (border_h, recv_a, a_ss, a_rs),
            (send_b, recv_b, b_ss, b_rs),
        )[which]
        return pltpu.make_async_remote_copy(
            source.at[d], landing.at[d], sent.at[d], received.at[d],
            device_id=sides[d][1], device_id_type=MESH,
        )

    for which in range(3):
        for d in range(4):
            @pl.when(sides[d][0])
            def _():
                border_copy(d, which).start()

    columns = volume[...].T * norm
    for i in range(ROWS // 2):
        volb[2 * i:2 * i + 2] = jnp.broadcast_to(columns[:, i:i + 1], (128, 128)).reshape(2, BS, 128)

    @pl.loop(0, STEPS)
    def _(step):
        own_copy(step).wait()
        for j in range(UNROLL):
            i = step * UNROLL + j
            gathered = jnp.concatenate([basis[own_cols[k, i]] for k in range(KOWN)], axis=0)
            sums[i] = lax.dot_general(
                own[i].reshape(KOWN * BS, 2 * BS), gathered, CONTRACT_FIRST, preferred_element_type=F32
            )

    for d, (may_send, _, may_receive) in enumerate(sides):
        @pl.when(may_receive)
        def _():
            border_copy(d, 0).wait_recv()
    targets = recv_rows[...].reshape(SLOTS, 128)
    slot = lax.broadcasted_iota(I32, (SLOTS, 128), 0)
    lane = lax.broadcasted_iota(I32, (SLOTS, 128), 1)
    target_lane = jnp.sum(jnp.where(slot == lane, targets, 0), axis=0, keepdims=True)
    target_lane = jnp.broadcast_to(target_lane, (SLOTS, 128))
    source = jnp.max(jnp.where(targets == lane, ROWS + slot, lane), axis=0, keepdims=True)
    base = jnp.max(
        jnp.where((targets == target_lane) & (slot < lane), ROWS + slot, target_lane), axis=0, keepdims=True
    )
    last = 1 - jnp.max(
        jnp.where((targets == target_lane) & (slot > lane), 1, 0), axis=0, keepdims=True
    )
    table_v[0:1, :] = source
    table_v[1:2, :] = base
    table_v[2:3, :] = last
    table_v[3:4, :] = target_lane[0:1]
    table_v[4:8, :] = jnp.zeros((4, 128), I32)
    table_copy = pltpu.make_async_copy(table_v, table, table_sem)
    table_copy.start()
    table_copy.wait()

    part[...] = jnp.zeros_like(part)

    def add_product(left, right):
        product = lax.dot_general(left, right, CONTRACT_FIRST, preferred_element_type=F32)
        for lanes in range(4):
            part[lanes] += product[:, lanes * 128:(lanes + 1) * 128]

    @pl.loop(0, ROWS // PROJ)
    def _(step):
        for j in range(PROJ):
            i = step * PROJ + j
            keep = jnp.where(table[0, i] == i, 1.0, 0.0).astype(F32)
            scale = volb[i] * keep
            scale = jnp.concatenate([scale, scale], axis=1)
            row = sums[i]
            w_chunk[j, :, 0:MODES] = (row[0:BS] * scale).astype(BF16)
            w_chunk[j, :, MODES:2 * MODES] = (row[BS:2 * BS] * scale).astype(BF16)
        left = basis[pl.ds(step * PROJ, PROJ)].reshape(PROJ * BS, MODES)
        add_product(left, w_chunk[...].reshape(PROJ * BS, 2 * MODES))

    for d, (_, _, may_receive) in enumerate(sides):
        @pl.when(may_receive)
        def _():
            border_copy(d, 1).wait_recv()
            border_copy(d, 2).wait_recv()

        for n in range(NB):
            m = d * NB + n
            partial = lax.dot_general(recv_a[d, n], recv_b[d, n], CONTRACT_FIRST, preferred_element_type=F32)
            total = sums[table[1, m]] + partial
            sums[ROWS + m] = total
            row = table[3, m]
            scale = volb[row] * table[2, m].astype(F32)
            scale = jnp.concatenate([scale, scale], axis=1)
            w_slot[n, :, 0:MODES] = (total[0:BS] * scale).astype(BF16)
            w_slot[n, :, MODES:2 * MODES] = (total[BS:2 * BS] * scale).astype(BF16)
        left = jnp.concatenate([basis[table[3, d * NB + n]] for n in range(NB)], axis=0)
        add_product(left, w_slot[...].reshape(NB * BS, 2 * MODES))

    for cc in range(2):
        for r in range(2):
            for lanes in range(4):
                for a in range(2):
                    for b in range(2):
                        q[cc, pl.ds((a * 2 + b) * 8 + lanes * 2 + r, 16, stride=32), :] = part[
                            lanes, pl.ds(a * 128 + b * 4 + 2 * cc + r, 16, stride=8), :
                        ]
    pair_copy = pltpu.make_async_remote_copy(
        q.at[1 - core], pair, pair_sem.at[0], pair_sem.at[1], device_id=mate, device_id_type=MESH
    )
    pair_copy.start()
    pair_copy.wait()
    h[...] = (q[core] + pair[...]).reshape(16, 32, 128)

    @pl.loop(1, 16)
    def _(k):
        to = yz_peer(k)
        pltpu.make_async_remote_copy(
            h.at[to[1] * 4 + to[2]], recv_yz.at[k], yz_sem.at[0], yz_sem.at[1],
            device_id=ident(to, core), device_id_type=MESH,
        ).start()

    @pl.loop(0, ROWS // 4)
    def _(step):
        for j in range(4):
            i = step * 4 + j
            row = sums[table[0, i]]
            applied_out[0, i] = row[0:BS].astype(BF16)
            applied_out[1, i] = row[BS:2 * BS].astype(BF16)

    pltpu.make_async_remote_copy(
        h.at[pl.ds(1, 15)], recv_yz.at[pl.ds(1, 15)], yz_sem.at[0], yz_sem.at[1],
        device_id=mate, device_id_type=MESH,
    ).wait()
    recv_yz[0] = h[y * 4 + z]
    h[0] = recv_yz[...].sum(axis=0)
    for k in range(1, 4):
        to = x_peer(k)
        block = pl.ds(pl.multiple_of((to[0] * 2 + to[3]) * 8, 8), 8)
        pltpu.make_async_remote_copy(
            h.at[0, block], recv_x.at[k], x_sem.at[0], x_sem.at[1],
            device_id=ident(to, core), device_id_type=MESH,
        ).start()
    pltpu.make_async_remote_copy(
        recv_x.at[pl.ds(1, 3)], recv_x.at[pl.ds(1, 3)], x_sem.at[0], x_sem.at[1],
        device_id=mate, device_id_type=MESH,
    ).wait()
    recv_x[0] = h[0, pl.ds(pl.multiple_of((xl * 2 + xh) * 8, 8), 8)]
    mine = recv_x[...].sum(axis=0)
    for r in range(2):
        for lanes in range(4):
            reduced_out[r, lanes // 2:lanes // 2 + 1, (lanes % 2) * 128:(lanes % 2 + 1) * 128] = mine[
                lanes * 2 + r:lanes * 2 + r + 1
            ]

    for d, (may_send, _, _) in enumerate(sides):
        @pl.when(may_send)
        def _():
            for which in range(3):
                border_copy(d, which).wait_send()


def local(basis, volume, own_blocks, own_cols, border_blocks, border_cols, border_rows):
    norm = 1.0 / math.sqrt(lax.axis_size("stream") * lax.axis_size("cross") * ROWS * BS)
    smem = pl.BlockSpec(memory_space=pltpu.SMEM)
    vmem = pl.BlockSpec(memory_space=pltpu.VMEM)
    anywhere = pl.BlockSpec(memory_space=pl.ANY)
    dma = pltpu.SemaphoreType.DMA
    applied, reduced = pl.pallas_call(
        functools.partial(kernel, norm),
        name="galerkin",
        in_specs=[smem, smem, smem, anywhere, vmem, anywhere, anywhere],
        out_specs=[vmem, vmem],
        out_shape=[
            jax.ShapeDtypeStruct((2, ROWS, BS, MODES), BF16),
            jax.ShapeDtypeStruct((2, 2, MODES), F32),
        ],
        scratch_shapes=[
            pltpu.VMEM((ROWS, KOWN, BS, 2 * BS), BF16),
            pltpu.VMEM((ROWS, BS, MODES), BF16),
            pltpu.VMEM((ROWS + SLOTS, 2 * BS, MODES), F32),
            pltpu.VMEM((ROWS, BS, 128), F32),
            pltpu.VMEM((4, NB, 128), I32),
            pltpu.VMEM((4, NB, BS, MODES), BF16),
            pltpu.VMEM((4, NB, 128), I32),
            pltpu.VMEM((4, NB, BS, 2 * BS), BF16),
            pltpu.VMEM((4, NB, BS, MODES), BF16),
            pltpu.VMEM((8, 128), I32),
            pltpu.SMEM((8, 128), I32),
            pltpu.VMEM((PROJ, BS, 2 * MODES), BF16),
            pltpu.VMEM((NB, BS, 2 * MODES), BF16),
            pltpu.VMEM((4, MODES, 128), F32),
            pltpu.VMEM((2, 512, 128), F32),
            pltpu.VMEM((512, 128), F32),
            pltpu.VMEM((16, 32, 128), F32),
            pltpu.VMEM((16, 32, 128), F32),
            pltpu.VMEM((4, 8, 128), F32),
            dma((STEPS,)), dma(()), dma(()),
            dma((4,)), dma((4,)), dma((4,)), dma((4,)), dma((4,)), dma((4,)),
            dma((2,)), dma((2,)), dma((2,)),
        ],
        compiler_params=pltpu.CompilerParams(
            collective_id=0, has_side_effects=True, vmem_limit_bytes=60 << 20
        ),
        cost_estimate=pl.CostEstimate(flops=4_700_000_000, bytes_accessed=21_000_000, transcendentals=0),
    )(
        own_cols.T,
        border_cols[0],
        border_rows[0],
        basis.reshape(ROWS, BS, MODES),
        volume.reshape(ROWS // 2, 128),
        own_blocks,
        border_blocks[0],
    )
    applied = applied.reshape(2, ROWS * BS, MODES)
    return applied, reduced


def solution(mesh):
    both = ("stream", "cross")
    return jax.shard_map(
        local,
        mesh=mesh,
        in_specs=(
            P(both, None), P(both), P(both, None, None, None), P(both, None),
            P(both, None, None, None, None), P(both, None, None), P(both, None, None),
        ),
        out_specs=(P(None, both, None), P(both, None, None)),
        check_vma=False,
    )
```

```python
import functools
import math

import jax
import jax.numpy as jnp
from jax import lax
from jax.experimental import pallas as pl
from jax.experimental.pallas import tpu as pltpu
from jax.sharding import PartitionSpec as P

MESH = pl.DeviceIdType.MESH
F32, BF16, I32 = jnp.float32, jnp.bfloat16, jnp.int32

ROWS = 96
KOWN = 7
BS = 64
MODES = 256
NB = 8
SLOTS = 4 * NB
UNROLL = 16
STEPS = ROWS // UNROLL
PROJ = 8

CONTRACT_FIRST = (((0,), (0,)), ((), ()))


def ident(chip, core):
    x, y, z = chip
    return ((x % 2) * 4 + y, z * 4 + (x // 2) * 2 + core)


def moved(chip, dx, dy, dz):
    x, y, z = chip
    return ((x + dx) % 4, (y + dy) % 4, (z + dz) % 4)


AROUND = ((1, 0, 0), (3, 0, 0), (0, 1, 0), (0, 3, 0), (0, 0, 1), (0, 0, 3))
ROUNDS = (AROUND, ((0, 3, 1), (0, 1, 1)), ((0, 3, 2), (2, 0, 0)))
ORDER = (2, 3, 0, 1)
HALF = NB // 2


def kernel(
    norm,
    own_cols, border_cols, border_rows,
    basis_h, volume, own_h, border_h,
    applied_out, reduced_out,
    own, basis, sums, volb, send_rows, send_b, recv_rows, recv_a, recv_b, relay_a, relay_b, table_v, table,
    w_chunk, w_slot, part, q, pair, h, recv_h,
    own_sem, basis_sem, table_sem, rows_ss, rows_rs, a_ss, a_rs, b_ss, b_rs,
    in_ss, in_rs, out_ss, pair_sem, all_sem, known,
):
    s, c = lax.axis_index("stream"), lax.axis_index("cross")
    x, y, z = chip = ((c // 2) % 2 * 2 + s // 4, s % 4, c // 4)
    core = c % 2
    mate = ident(chip, 1 - core)

    def tell(number):
        for step in ROUNDS[number]:
            pl.semaphore_signal(known.at[number], inc=1, device_id=ident(moved(chip, *step), core), device_id_type=MESH)

    def told(number):
        pl.semaphore_wait(known.at[number], len(ROUNDS[number]))

    sides = [
        (c < 15, (s, c + 1), c > 0),
        (c > 0, (s, c - 1), c < 15),
        (s < 7, (s + 1, c), s > 0),
        (s > 0, (s - 1, c), s < 7),
    ]
    corners = ((2, 3, 0, 4), (3, 4, 7, 3))

    basis_copy = pltpu.make_async_copy(basis_h, basis, basis_sem)
    basis_copy.start()

    def own_copy(step):
        rows = pl.ds(step * UNROLL, UNROLL)
        return pltpu.make_async_copy(own_h.at[rows], own.at[rows], own_sem.at[step])

    barrier = pltpu.get_barrier_semaphore()
    for may_send, target, _ in sides:
        @pl.when(may_send)
        def _():
            pl.semaphore_signal(barrier, inc=1, device_id=target, device_id_type=MESH)
    pl.semaphore_signal(barrier, inc=1, device_id=mate, device_id_type=MESH)

    for step in AROUND:
        pl.semaphore_signal(barrier, inc=1, device_id=ident(moved(chip, *step), core), device_id_type=MESH)

    for step in range(STEPS):
        own_copy(step).start()

    for d in range(4):
        for n in range(NB):
            send_rows[d, pl.ds(n, 1), :] = jnp.full((1, 128), border_rows[ORDER[d], n], I32)
    for d, (_, _, may_receive) in enumerate(sides):
        @pl.when(jnp.logical_not(may_receive))
        def _():
            recv_rows[d] = jnp.zeros((NB, 128), I32)
            recv_a[d] = jnp.zeros((NB, BS, 2 * BS), BF16)
            recv_b[d] = jnp.zeros((NB, BS, MODES), BF16)

    basis_copy.wait()
    for d in range(4):
        for n in range(NB):
            send_b[d, n] = basis[border_cols[ORDER[d], n]]

    greeted = sum(jnp.where(may_receive, 1, 0) for _, _, may_receive in sides)
    pl.semaphore_wait(barrier, greeted + 1 + len(AROUND))

    tell(0)

    def rows_copy(d):
        return pltpu.make_async_remote_copy(
            send_rows.at[d], recv_rows.at[d], rows_ss.at[d], rows_rs.at[d], device_id=sides[d][1], device_id_type=MESH
        )

    def half_copies(d, half):
        blocks = pl.ds(half * HALF, HALF)
        return (
            pltpu.make_async_remote_copy(
                border_h.at[ORDER[d], blocks], recv_a.at[d, blocks], a_ss.at[d, half], a_rs.at[d, half],
                device_id=sides[d][1], device_id_type=MESH,
            ),
            pltpu.make_async_remote_copy(
                send_b.at[d, blocks], recv_b.at[d, blocks], b_ss.at[d, half], b_rs.at[d, half],
                device_id=sides[d][1], device_id_type=MESH,
            ),
        )

    def corner_copies(d, corner, k):
        return (
            pltpu.make_async_remote_copy(
                border_h.at[ORDER[d], HALF + k], relay_a.at[k], in_ss.at[0, k], in_rs.at[0, k],
                device_id=(corner, c), device_id_type=MESH,
            ),
            pltpu.make_async_remote_copy(
                send_b.at[d, HALF + k], relay_b.at[k], in_ss.at[1, k], in_rs.at[1, k],
                device_id=(corner, c), device_id_type=MESH,
            ),
        )

    def onward_copies(d, receiver, k):
        return (
            pltpu.make_async_remote_copy(
                relay_a.at[k], recv_a.at[d, HALF + k], out_ss.at[0, k], a_rs.at[d, 1],
                device_id=(receiver, c), device_id_type=MESH,
            ),
            pltpu.make_async_remote_copy(
                relay_b.at[k], recv_b.at[d, HALF + k], out_ss.at[1, k], b_rs.at[d, 1],
                device_id=(receiver, c), device_id_type=MESH,
            ),
        )

    for d in range(4):
        @pl.when(sides[d][0])
        def _():
            rows_copy(d).start()
    by_corner = {d: (sender, corner) for d, sender, corner, _ in corners}
    for d, (sender, corner) in by_corner.items():
        @pl.when(s == sender)
        def _():
            for k in range(HALF):
                for copy in corner_copies(d, corner, k):
                    copy.start()
    for half in (0, 1):
        for d in (2, 3, 0, 1):
            direct = sides[d][0]
            if half and d in by_corner:
                direct = jnp.logical_and(direct, s != by_corner[d][0])

            @pl.when(direct)
            def _():
                for copy in half_copies(d, half):
                    copy.start()

    columns = volume[...].T * norm
    for i in range(ROWS // 2):
        volb[2 * i:2 * i + 2] = jnp.broadcast_to(columns[:, i:i + 1], (128, 128)).reshape(2, BS, 128)

    @pl.loop(0, STEPS)
    def _(step):
        own_copy(step).wait()
        for d, _, corner, receiver in corners:
            @pl.when(jnp.logical_and(step >= STEPS - HALF, s == corner))
            def _():
                k = step - (STEPS - HALF)
                for copy in corner_copies(d, corner, k):
                    copy.wait_recv()
                for copy in onward_copies(d, receiver, k):
                    copy.start()

        @pl.when(step == 2)
        def _():
            told(0)
            tell(1)

        @pl.when(step == 4)
        def _():
            told(1)
            tell(2)

        for j in range(UNROLL):
            i = step * UNROLL + j
            gathered = jnp.concatenate([basis[own_cols[k, i]] for k in range(KOWN)], axis=0)
            sums[i] = lax.dot_general(
                own[i].reshape(KOWN * BS, 2 * BS), gathered, CONTRACT_FIRST, preferred_element_type=F32
            )

    for d, (may_send, _, may_receive) in enumerate(sides):
        @pl.when(may_receive)
        def _():
            rows_copy(d).wait_recv()
    targets = recv_rows[...].reshape(SLOTS, 128)
    slot = lax.broadcasted_iota(I32, (SLOTS, 128), 0)
    lane = lax.broadcasted_iota(I32, (SLOTS, 128), 1)
    target_lane = jnp.sum(jnp.where(slot == lane, targets, 0), axis=0, keepdims=True)
    target_lane = jnp.broadcast_to(target_lane, (SLOTS, 128))
    source = jnp.max(jnp.where(targets == lane, ROWS + slot, lane), axis=0, keepdims=True)
    base = jnp.max(
        jnp.where((targets == target_lane) & (slot < lane), ROWS + slot, target_lane), axis=0, keepdims=True
    )
    last = 1 - jnp.max(
        jnp.where((targets == target_lane) & (slot > lane), 1, 0), axis=0, keepdims=True
    )
    table_v[0:1, :] = source
    table_v[1:2, :] = base
    table_v[2:3, :] = last
    table_v[3:4, :] = target_lane[0:1]
    table_v[4:8, :] = jnp.zeros((4, 128), I32)
    table_copy = pltpu.make_async_copy(table_v, table, table_sem)
    table_copy.start()
    table_copy.wait()

    part[...] = jnp.zeros_like(part)

    def add_product(left, right):
        product = lax.dot_general(left, right, CONTRACT_FIRST, preferred_element_type=F32)
        for lanes in range(4):
            part[lanes] += product[:, lanes * 128:(lanes + 1) * 128]

    @pl.loop(0, ROWS // PROJ)
    def _(step):
        for j in range(PROJ):
            i = step * PROJ + j
            keep = jnp.where(table[0, i] == i, 1.0, 0.0).astype(F32)
            scale = volb[i] * keep
            scale = jnp.concatenate([scale, scale], axis=1)
            row = sums[i]
            w_chunk[j, :, 0:MODES] = (row[0:BS] * scale).astype(BF16)
            w_chunk[j, :, MODES:2 * MODES] = (row[BS:2 * BS] * scale).astype(BF16)
        left = basis[pl.ds(step * PROJ, PROJ)].reshape(PROJ * BS, MODES)
        add_product(left, w_chunk[...].reshape(PROJ * BS, 2 * MODES))

    for part_at in range(8):
        d, half = part_at // 2, part_at % 2

        @pl.when(sides[d][2])
        def _():
            for copy in half_copies(d, half):
                copy.wait_recv()

        first = d * NB + half * HALF
        for j in range(HALF):
            n = half * HALF + j
            m = first + j
            partial = lax.dot_general(recv_a[d, n], recv_b[d, n], CONTRACT_FIRST, preferred_element_type=F32)
            total = sums[table[1, m]] + partial
            sums[ROWS + m] = total
            row = table[3, m]
            scale = volb[row] * table[2, m].astype(F32)
            scale = jnp.concatenate([scale, scale], axis=1)
            w_slot[j, :, 0:MODES] = (total[0:BS] * scale).astype(BF16)
            w_slot[j, :, MODES:2 * MODES] = (total[BS:2 * BS] * scale).astype(BF16)
        left = jnp.concatenate([basis[table[3, first + j]] for j in range(HALF)], axis=0)
        add_product(left, w_slot[...].reshape(HALF * BS, 2 * MODES))

    told(2)

    for cc in range(2):
        for r in range(2):
            for lanes in range(4):
                for at in range(4):
                    q[cc, pl.ds(at * 128 + lanes * 2 + r, 16, stride=8), :] = part[
                        lanes, pl.ds((at % 2) * 128 + (at // 2) * 4 + 2 * cc + r, 16, stride=8), :
                    ]
    pair_copy = pltpu.make_async_remote_copy(
        q.at[1 - core], pair, pair_sem.at[0], pair_sem.at[1], device_id=mate, device_id_type=MESH
    )
    pair_copy.start()
    pair_copy.wait()
    h[...] = (q[core] + pair[...]).reshape(64, 8, 128)

    @pl.loop(1, 64)
    def _(k):
        to = moved(chip, k // 16, (k // 4) % 4, k % 4)
        pltpu.make_async_remote_copy(
            h.at[to[0] * 16 + to[1] * 4 + to[2]], recv_h.at[k], all_sem.at[0], all_sem.at[1],
            device_id=ident(to, core), device_id_type=MESH,
        ).start()

    @pl.loop(0, ROWS // 4)
    def _(step):
        for j in range(4):
            i = step * 4 + j
            row = sums[table[0, i]]
            applied_out[0, i] = row[0:BS].astype(BF16)
            applied_out[1, i] = row[BS:2 * BS].astype(BF16)

    pltpu.make_async_remote_copy(
        h.at[pl.ds(1, 63)], recv_h.at[pl.ds(1, 63)], all_sem.at[0], all_sem.at[1], device_id=mate, device_id_type=MESH
    ).wait()
    recv_h[0] = h[x * 16 + y * 4 + z]
    mine = recv_h[...].sum(axis=0)
    for r in range(2):
        for lanes in range(4):
            reduced_out[r, lanes // 2:lanes // 2 + 1, (lanes % 2) * 128:(lanes % 2 + 1) * 128] = mine[
                lanes * 2 + r:lanes * 2 + r + 1
            ]

    for d, (may_send, _, _) in enumerate(sides):
        @pl.when(may_send)
        def _():
            rows_copy(d).wait_send()
            for copy in half_copies(d, 0):
                copy.wait_send()

        direct = may_send
        if d in by_corner:
            direct = jnp.logical_and(may_send, s != by_corner[d][0])

        @pl.when(direct)
        def _():
            for copy in half_copies(d, 1):
                copy.wait_send()
    for d, sender, corner, receiver in corners:
        @pl.when(s == sender)
        def _():
            for k in range(HALF):
                for copy in corner_copies(d, corner, k):
                    copy.wait_send()

        @pl.when(s == corner)
        def _():
            for k in range(HALF):
                for copy in onward_copies(d, receiver, k):
                    copy.wait_send()


def local(basis, volume, own_blocks, own_cols, border_blocks, border_cols, border_rows):
    norm = 1.0 / math.sqrt(lax.axis_size("stream") * lax.axis_size("cross") * ROWS * BS)
    smem = pl.BlockSpec(memory_space=pltpu.SMEM)
    vmem = pl.BlockSpec(memory_space=pltpu.VMEM)
    anywhere = pl.BlockSpec(memory_space=pl.ANY)
    dma = pltpu.SemaphoreType.DMA
    applied, reduced = pl.pallas_call(
        functools.partial(kernel, norm),
        name="galerkin",
        in_specs=[smem, smem, smem, anywhere, vmem, anywhere, anywhere],
        out_specs=[vmem, vmem],
        out_shape=[
            pltpu.VMEM((2, ROWS, BS, MODES), BF16),
            pltpu.VMEM((2, 2, MODES), F32),
        ],
        scratch_shapes=[
            pltpu.VMEM((ROWS, KOWN, BS, 2 * BS), BF16),
            pltpu.VMEM((ROWS, BS, MODES), BF16),
            pltpu.VMEM((ROWS + SLOTS, 2 * BS, MODES), F32),
            pltpu.VMEM((ROWS, BS, 128), F32),
            pltpu.VMEM((4, NB, 128), I32),
            pltpu.VMEM((4, NB, BS, MODES), BF16),
            pltpu.VMEM((4, NB, 128), I32),
            pltpu.VMEM((4, NB, BS, 2 * BS), BF16),
            pltpu.VMEM((4, NB, BS, MODES), BF16),
            pltpu.VMEM((HALF, BS, 2 * BS), BF16),
            pltpu.VMEM((HALF, BS, MODES), BF16),
            pltpu.VMEM((8, 128), I32),
            pltpu.SMEM((8, 128), I32),
            pltpu.VMEM((PROJ, BS, 2 * MODES), BF16),
            pltpu.VMEM((HALF, BS, 2 * MODES), BF16),
            pltpu.VMEM((4, MODES, 128), F32),
            pltpu.VMEM((2, 512, 128), F32),
            pltpu.VMEM((512, 128), F32),
            pltpu.VMEM((64, 8, 128), F32),
            pltpu.VMEM((64, 8, 128), F32),
            dma((STEPS,)), dma(()), dma(()),
            dma((4,)), dma((4,)), dma((4, 2)), dma((4, 2)), dma((4, 2)), dma((4, 2)),
            dma((2, HALF)), dma((2, HALF)), dma((2, HALF)),
            dma((2,)), dma((2,)), pltpu.SemaphoreType.REGULAR((len(ROUNDS),)),
        ],
        compiler_params=pltpu.CompilerParams(
            collective_id=0, has_side_effects=True, vmem_limit_bytes=48 << 20
        ),
        cost_estimate=pl.CostEstimate(flops=4_700_000_000, bytes_accessed=21_000_000, transcendentals=0),
    )(
        own_cols.T,
        border_cols[0],
        border_rows[0],
        basis.reshape(ROWS, BS, MODES),
        volume.reshape(ROWS // 2, 128),
        own_blocks,
        border_blocks[0],
    )
    applied = applied.reshape(2, ROWS * BS, MODES)
    return applied, reduced


def solution(mesh):
    both = ("stream", "cross")
    return jax.shard_map(
        local,
        mesh=mesh,
        in_specs=(
            P(both, None), P(both), P(both, None, None, None), P(both, None),
            P(both, None, None, None, None), P(both, None, None), P(both, None, None),
        ),
        out_specs=(P(None, both, None), P(both, None, None)),
        check_vma=False,
    )
```

```python
import functools
import math

import jax
import jax.numpy as jnp
from jax import lax
from jax.experimental import pallas as pl
from jax.experimental.pallas import tpu as pltpu
from jax.sharding import PartitionSpec as P

MESH = pl.DeviceIdType.MESH
F32, BF16, I32 = jnp.float32, jnp.bfloat16, jnp.int32

ROWS = 96
KOWN = 7
BS = 64
MODES = 256
NB = 8
SLOTS = 4 * NB
UNROLL = 16
STEPS = ROWS // UNROLL
PROJ = 8

CONTRACT_FIRST = (((0,), (0,)), ((), ()))


def ident(chip, core):
    x, y, z = chip
    return ((x % 2) * 4 + y, z * 4 + (x // 2) * 2 + core)


def moved(chip, dx, dy, dz):
    x, y, z = chip
    return ((x + dx) % 4, (y + dy) % 4, (z + dz) % 4)


AROUND = ((1, 0, 0), (3, 0, 0), (0, 1, 0), (0, 3, 0), (0, 0, 1), (0, 0, 3))
ROUNDS = (AROUND, ((0, 3, 1), (0, 1, 1)), ((0, 3, 2), (2, 0, 0)))
ORDER = (2, 3, 0, 1)
HALF = NB // 2


def kernel(
    norm,
    own_cols_h, border_cols_h, border_rows_h, basis_h, volume_h, own_h, border_h,
    applied_out, reduced_out,
    own_cols, border_cols, border_rows, volume,
    own, basis, sums, volb, send_rows, send_b, recv_rows, recv_a, recv_b, relay_a, relay_b, table_v, table,
    w_chunk, w_slot, part, q, pair, h, recv_h,
    own_sem, basis_sem, small_sem, table_sem, rows_ss, rows_rs, a_ss, a_rs, b_ss, b_rs,
    in_ss, in_rs, out_ss, pair_ss, pair_rs, all_sem, known,
):
    s, c = lax.axis_index("stream"), lax.axis_index("cross")
    x, y, z = chip = ((c // 2) % 2 * 2 + s // 4, s % 4, c // 4)
    core = c % 2
    mate = ident(chip, 1 - core)

    def tell(number):
        for step in ROUNDS[number]:
            pl.semaphore_signal(known.at[number], inc=1, device_id=ident(moved(chip, *step), core), device_id_type=MESH)

    def told(number):
        pl.semaphore_wait(known.at[number], len(ROUNDS[number]))

    sides = [
        (c < 15, (s, c + 1), c > 0),
        (c > 0, (s, c - 1), c < 15),
        (s < 7, (s + 1, c), s > 0),
        (s > 0, (s - 1, c), s < 7),
    ]
    lands = (0, 1, jnp.where(s == 3, 3, 2), jnp.where(s == 5, 2, 3))
    corners = ((2, 3, 0, 4), (3, 4, 7, 3))

    small_copies = [
        pltpu.make_async_copy(source, landing, small_sem.at[i])
        for i, (source, landing) in enumerate((
            (border_cols_h, border_cols), (border_rows_h, border_rows), (own_cols_h, own_cols), (volume_h, volume),
        ))
    ]
    small_copies[0].start()
    small_copies[1].start()
    basis_copy = pltpu.make_async_copy(basis_h, basis, basis_sem)
    basis_copy.start()

    def own_copy(step):
        rows = pl.ds(step * UNROLL, UNROLL)
        return pltpu.make_async_copy(own_h.at[rows], own.at[rows], own_sem.at[step])

    barrier = pltpu.get_barrier_semaphore()
    for may_send, target, _ in sides:
        @pl.when(may_send)
        def _():
            pl.semaphore_signal(barrier, inc=1, device_id=target, device_id_type=MESH)
    pl.semaphore_signal(barrier, inc=1, device_id=mate, device_id_type=MESH)

    for step in AROUND:
        pl.semaphore_signal(barrier, inc=1, device_id=ident(moved(chip, *step), core), device_id_type=MESH)

    for copy in small_copies[2:]:
        copy.start()

    for d, (_, _, may_receive) in enumerate(sides):
        @pl.when(jnp.logical_not(may_receive))
        def _():
            recv_rows[d] = jnp.zeros((NB, 128), I32)
            recv_a[d] = jnp.zeros((NB, BS, 2 * BS), BF16)
            recv_b[d] = jnp.zeros((NB, BS, MODES), BF16)

    small_copies[1].wait()
    for d in range(4):
        for n in range(NB):
            send_rows[d, pl.ds(n, 1), :] = jnp.full((1, 128), border_rows[ORDER[d], n], I32)
    greeted = sum(jnp.where(may_receive, 1, 0) for _, _, may_receive in sides)
    pl.semaphore_wait(barrier, greeted + 1 + len(AROUND))

    def rows_copy(d, land):
        return pltpu.make_async_remote_copy(
            send_rows.at[d], recv_rows.at[land], rows_ss.at[d], rows_rs.at[land],
            device_id=sides[d][1], device_id_type=MESH,
        )

    def half_copies(d, half, land):
        blocks = pl.ds(half * HALF, HALF)
        return (
            pltpu.make_async_remote_copy(
                border_h.at[ORDER[d], blocks], recv_a.at[land, blocks], a_ss.at[d, half], a_rs.at[land, half],
                device_id=sides[d][1], device_id_type=MESH,
            ),
            pltpu.make_async_remote_copy(
                send_b.at[d, blocks], recv_b.at[land, blocks], b_ss.at[d, half], b_rs.at[land, half],
                device_id=sides[d][1], device_id_type=MESH,
            ),
        )

    def corner_copies(d, corner, k):
        return (
            pltpu.make_async_remote_copy(
                border_h.at[ORDER[d], HALF + k], relay_a.at[k], in_ss.at[0, k], in_rs.at[0, k],
                device_id=(corner, c), device_id_type=MESH,
            ),
            pltpu.make_async_remote_copy(
                send_b.at[d, HALF + k], relay_b.at[k], in_ss.at[1, k], in_rs.at[1, k],
                device_id=(corner, c), device_id_type=MESH,
            ),
        )

    def onward_copies(receiver, k):
        return (
            pltpu.make_async_remote_copy(
                relay_a.at[k], recv_a.at[3, HALF + k], out_ss.at[0, k], a_rs.at[3, 1],
                device_id=(receiver, c), device_id_type=MESH,
            ),
            pltpu.make_async_remote_copy(
                relay_b.at[k], recv_b.at[3, HALF + k], out_ss.at[1, k], b_rs.at[3, 1],
                device_id=(receiver, c), device_id_type=MESH,
            ),
        )

    by_corner = {d: (sender, corner) for d, sender, corner, _ in corners}

    def send(d, which):
        @pl.when(sides[d][0])
        def _():
            half_copies(d, 0, lands[d])[which].start()

        if d not in by_corner:
            @pl.when(sides[d][0])
            def _():
                half_copies(d, 1, lands[d])[which].start()

            return
        sender, corner = by_corner[d]

        @pl.when(s == sender)
        def _():
            for k in range(HALF):
                corner_copies(d, corner, k)[which].start()

        @pl.when(jnp.logical_and(sides[d][0], s != sender))
        def _():
            half_copies(d, 1, lands[d])[which].start()

    for d in range(4):
        @pl.when(sides[d][0])
        def _():
            rows_copy(d, lands[d]).start()

    for d in (2, 3, 0, 1):
        send(d, 0)
    small_copies[0].wait()
    basis_copy.wait()
    for d in (2, 3, 0, 1):
        for n in range(NB):
            send_b[d, n] = basis[border_cols[ORDER[d], n]]
        send(d, 1)
    for step in range(STEPS):
        own_copy(step).start()
    tell(0)
    small_copies[2].wait()
    small_copies[3].wait()

    columns = volume[...].T * norm
    for i in range(ROWS // 2):
        volb[2 * i:2 * i + 2] = jnp.broadcast_to(columns[:, i:i + 1], (128, 128)).reshape(2, BS, 128)

    @pl.loop(0, STEPS)
    def _(step):
        own_copy(step).wait()
        for d, _, corner, receiver in corners:
            @pl.when(jnp.logical_and(step >= STEPS - HALF, s == corner))
            def _():
                k = step - (STEPS - HALF)
                for copy in corner_copies(d, corner, k):
                    copy.wait_recv()
                for copy in onward_copies(receiver, k):
                    copy.start()

        @pl.when(step == 2)
        def _():
            told(0)
            tell(1)

        @pl.when(step == 4)
        def _():
            told(1)
            tell(2)

        for j in range(UNROLL):
            i = step * UNROLL + j
            gathered = jnp.concatenate([basis[own_cols[k, i]] for k in range(KOWN)], axis=0)
            sums[i] = lax.dot_general(
                own[i].reshape(KOWN * BS, 2 * BS), gathered, CONTRACT_FIRST, preferred_element_type=F32
            )

    for d, (may_send, _, may_receive) in enumerate(sides):
        @pl.when(may_receive)
        def _():
            rows_copy(d, d).wait_recv()
    targets = recv_rows[...].reshape(SLOTS, 128)
    slot = lax.broadcasted_iota(I32, (SLOTS, 128), 0)
    lane = lax.broadcasted_iota(I32, (SLOTS, 128), 1)
    target_lane = jnp.sum(jnp.where(slot == lane, targets, 0), axis=0, keepdims=True)
    target_lane = jnp.broadcast_to(target_lane, (SLOTS, 128))
    source = jnp.max(jnp.where(targets == lane, ROWS + slot, lane), axis=0, keepdims=True)
    base = jnp.max(
        jnp.where((targets == target_lane) & (slot < lane), ROWS + slot, target_lane), axis=0, keepdims=True
    )
    last = 1 - jnp.max(
        jnp.where((targets == target_lane) & (slot > lane), 1, 0), axis=0, keepdims=True
    )
    table_v[0:1, :] = source
    table_v[1:2, :] = base
    table_v[2:3, :] = last
    table_v[3:4, :] = target_lane[0:1]
    table_v[4:8, :] = jnp.zeros((4, 128), I32)
    table_copy = pltpu.make_async_copy(table_v, table, table_sem)
    table_copy.start()
    table_copy.wait()

    part[...] = jnp.zeros_like(part)

    def add_product(left, right):
        product = lax.dot_general(left, right, CONTRACT_FIRST, preferred_element_type=F32)
        for lanes in range(4):
            part[lanes] += product[:, lanes * 128:(lanes + 1) * 128]

    @pl.loop(0, ROWS // PROJ)
    def _(step):
        for j in range(PROJ):
            i = step * PROJ + j
            keep = jnp.where(table[0, i] == i, 1.0, 0.0).astype(F32)
            scale = volb[i] * keep
            scale = jnp.concatenate([scale, scale], axis=1)
            row = sums[i]
            w_chunk[j, :, 0:MODES] = (row[0:BS] * scale).astype(BF16)
            w_chunk[j, :, MODES:2 * MODES] = (row[BS:2 * BS] * scale).astype(BF16)
        left = basis[pl.ds(step * PROJ, PROJ)].reshape(PROJ * BS, MODES)
        add_product(left, w_chunk[...].reshape(PROJ * BS, 2 * MODES))

    for d in range(4):
        @pl.when(sides[d][2])
        def _():
            for half in range(2):
                for copy in half_copies(d, half, d):
                    copy.wait_recv()

        for n in range(NB):
            m = d * NB + n
            partial = lax.dot_general(recv_a[d, n], recv_b[d, n], CONTRACT_FIRST, preferred_element_type=F32)
            total = sums[table[1, m]] + partial
            sums[ROWS + m] = total
            row = table[3, m]
            scale = volb[row] * table[2, m].astype(F32)
            scale = jnp.concatenate([scale, scale], axis=1)
            w_slot[n, :, 0:MODES] = (total[0:BS] * scale).astype(BF16)
            w_slot[n, :, MODES:2 * MODES] = (total[BS:2 * BS] * scale).astype(BF16)
        left = jnp.concatenate([basis[table[3, d * NB + n]] for n in range(NB)], axis=0)
        add_product(left, w_slot[...].reshape(NB * BS, 2 * MODES))

    told(2)

    for cc in range(2):
        for r in range(2):
            for lanes in range(4):
                for at in range(4):
                    q[cc, pl.ds(at * 128 + lanes * 2 + r, 16, stride=8), :] = part[
                        lanes, pl.ds((at % 2) * 128 + (at // 2) * 4 + 2 * cc + r, 16, stride=8), :
                    ]
    order = [(x + i) % 4 for i in (2, 1, 3, 0)]

    def pair_copy(i):
        tiles = pl.ds(pl.multiple_of(order[i] * 128, 128), 128)
        return pltpu.make_async_remote_copy(
            q.at[1 - core, tiles], pair.at[tiles], pair_ss.at[i], pair_rs.at[i], device_id=mate, device_id_type=MESH
        )

    def sum_copy(i, j):
        from_it = (x - order[i] + 4) % 4 * 16 + (y - j // 4 + 4) % 4 * 4 + (z - j % 4 + 4) % 4
        return from_it, pltpu.make_async_remote_copy(
            h.at[order[i] * 16 + j], recv_h.at[from_it], all_sem.at[0], all_sem.at[1],
            device_id=ident((order[i], j // 4, j % 4), core), device_id_type=MESH,
        )

    for i in range(4):
        pair_copy(i).start()
    for i in range(4):
        pair_copy(i).wait()
        tiles = pl.ds(pl.multiple_of(order[i] * 128, 128), 128)
        h[pl.ds(order[i] * 16, 16)] = (q[core, tiles] + pair[tiles]).reshape(16, 8, 128)

        @pl.loop(0, 16)
        def _(j):
            from_it, copy = sum_copy(i, j)

            @pl.when(from_it != 0)
            def _():
                copy.start()

    @pl.loop(0, ROWS // 4)
    def _(step):
        for j in range(4):
            i = step * 4 + j
            row = sums[table[0, i]]
            applied_out[0, i] = row[0:BS].astype(BF16)
            applied_out[1, i] = row[BS:2 * BS].astype(BF16)

    pltpu.make_async_remote_copy(
        h.at[pl.ds(1, 63)], recv_h.at[pl.ds(1, 63)], all_sem.at[0], all_sem.at[1], device_id=mate, device_id_type=MESH
    ).wait()
    recv_h[0] = h[x * 16 + y * 4 + z]
    mine = recv_h[...].sum(axis=0)
    for r in range(2):
        for lanes in range(4):
            reduced_out[r, lanes // 2:lanes // 2 + 1, (lanes % 2) * 128:(lanes % 2 + 1) * 128] = mine[
                lanes * 2 + r:lanes * 2 + r + 1
            ]

    for d, (may_send, _, _) in enumerate(sides):
        @pl.when(may_send)
        def _():
            rows_copy(d, d).wait_send()
            for copy in half_copies(d, 0, d):
                copy.wait_send()

        direct = may_send
        if d in by_corner:
            direct = jnp.logical_and(may_send, s != by_corner[d][0])

        @pl.when(direct)
        def _():
            for copy in half_copies(d, 1, d):
                copy.wait_send()
    for d, sender, corner, receiver in corners:
        @pl.when(s == sender)
        def _():
            for k in range(HALF):
                for copy in corner_copies(d, corner, k):
                    copy.wait_send()

        @pl.when(s == corner)
        def _():
            for k in range(HALF):
                for copy in onward_copies(receiver, k):
                    copy.wait_send()


def local(basis, volume, own_blocks, own_cols, border_blocks, border_cols, border_rows):
    norm = 1.0 / math.sqrt(lax.axis_size("stream") * lax.axis_size("cross") * ROWS * BS)
    vmem = pl.BlockSpec(memory_space=pltpu.VMEM)
    anywhere = pl.BlockSpec(memory_space=pl.ANY)
    dma = pltpu.SemaphoreType.DMA
    applied, reduced = pl.pallas_call(
        functools.partial(kernel, norm),
        name="galerkin",
        in_specs=[anywhere] * 7,
        out_specs=[vmem, vmem],
        out_shape=[
            pltpu.VMEM((2, ROWS, BS, MODES), BF16),
            pltpu.VMEM((2, 2, MODES), F32),
        ],
        scratch_shapes=[
            pltpu.SMEM((KOWN, ROWS), I32),
            pltpu.SMEM((4, NB), I32),
            pltpu.SMEM((4, NB), I32),
            pltpu.VMEM((ROWS // 2, 128), F32),
            pltpu.VMEM((ROWS, KOWN, BS, 2 * BS), BF16),
            pltpu.VMEM((ROWS, BS, MODES), BF16),
            pltpu.VMEM((ROWS + SLOTS, 2 * BS, MODES), F32),
            pltpu.VMEM((ROWS, BS, 128), F32),
            pltpu.VMEM((4, NB, 128), I32),
            pltpu.VMEM((4, NB, BS, MODES), BF16),
            pltpu.VMEM((4, NB, 128), I32),
            pltpu.VMEM((4, NB, BS, 2 * BS), BF16),
            pltpu.VMEM((4, NB, BS, MODES), BF16),
            pltpu.VMEM((HALF, BS, 2 * BS), BF16),
            pltpu.VMEM((HALF, BS, MODES), BF16),
            pltpu.VMEM((8, 128), I32),
            pltpu.SMEM((8, 128), I32),
            pltpu.VMEM((PROJ, BS, 2 * MODES), BF16),
            pltpu.VMEM((NB, BS, 2 * MODES), BF16),
            pltpu.VMEM((4, MODES, 128), F32),
            pltpu.VMEM((2, 512, 128), F32),
            pltpu.VMEM((512, 128), F32),
            pltpu.VMEM((64, 8, 128), F32),
            pltpu.VMEM((64, 8, 128), F32),
            dma((STEPS,)), dma(()), dma((4,)), dma(()),
            dma((4,)), dma((4,)), dma((4, 2)), dma((4, 2)), dma((4, 2)), dma((4, 2)),
            dma((2, HALF)), dma((2, HALF)), dma((2, HALF)),
            dma((4,)), dma((4,)), dma((2,)), pltpu.SemaphoreType.REGULAR((len(ROUNDS),)),
        ],
        compiler_params=pltpu.CompilerParams(
            collective_id=0, has_side_effects=True, vmem_limit_bytes=48 << 20
        ),
        cost_estimate=pl.CostEstimate(flops=4_700_000_000, bytes_accessed=21_000_000, transcendentals=0),
    )(
        own_cols.T,
        border_cols[0],
        border_rows[0],
        basis.reshape(ROWS, BS, MODES),
        volume.reshape(ROWS // 2, 128),
        own_blocks,
        border_blocks[0],
    )
    applied = applied.reshape(2, ROWS * BS, MODES)
    return applied, reduced


def solution(mesh):
    both = ("stream", "cross")
    return jax.shard_map(
        local,
        mesh=mesh,
        in_specs=(
            P(both, None), P(both), P(both, None, None, None), P(both, None),
            P(both, None, None, None, None), P(both, None, None), P(both, None, None),
        ),
        out_specs=(P(None, both, None), P(both, None, None)),
        check_vma=False,
    )
```

```python
import functools
import math

import jax
import jax.numpy as jnp
from jax import lax
from jax.experimental import pallas as pl
from jax.experimental.pallas import tpu as pltpu
from jax.sharding import PartitionSpec as P

MESH = pl.DeviceIdType.MESH
F32, BF16, I32 = jnp.float32, jnp.bfloat16, jnp.int32

ROWS = 96
KOWN = 7
BS = 64
MODES = 256
NB = 8
SLOTS = 4 * NB
UNROLL = 16
STEPS = ROWS // UNROLL
PROJ = 8

CONTRACT_FIRST = (((0,), (0,)), ((), ()))


def ident(chip, core):
    x, y, z = chip
    return ((x % 2) * 4 + y, z * 4 + (x // 2) * 2 + core)


def moved(chip, dx, dy, dz):
    x, y, z = chip
    return ((x + dx) % 4, (y + dy) % 4, (z + dz) % 4)


AROUND = ((1, 0, 0), (3, 0, 0), (0, 1, 0), (0, 3, 0), (0, 0, 1), (0, 0, 3))
ROUNDS = (AROUND, ((2, 0, 0), (0, 2, 0)), ((2, 1, 0), (0, 0, 2)))
ORDER = (2, 3, 0, 1)
HALF = NB // 2
DETOUR = 2


def kernel(
    norm,
    own_cols_h, border_cols_h, border_rows_h, basis_h, volume_h, own_h, border_h,
    applied_out, recv_h,
    own_cols, border_cols, border_rows, volume,
    own, basis, sums, volb, send_rows, send_b, recv_rows, recv_a, recv_b, relay_a, relay_b, side_a, side_b, table_v, table,
    w_chunk, w_slot, part, q, pair, h,
    own_sem, basis_sem, small_sem, table_sem, rows_ss, rows_rs, a_ss, a_rs, b_ss, b_rs,
    in_ss, in_rs, out_ss, side_ss, side_rs, side_out_ss, pair_ss, pair_rs, all_sem, known,
):
    s, c = lax.axis_index("stream"), lax.axis_index("cross")
    x, y, z = chip = ((c // 2) % 2 * 2 + s // 4, s % 4, c // 4)
    core = c % 2
    mate = ident(chip, 1 - core)

    def tell(number):
        for step in ROUNDS[number]:
            pl.semaphore_signal(known.at[number], inc=1, device_id=ident(moved(chip, *step), core), device_id_type=MESH)

    def told(number):
        pl.semaphore_wait(known.at[number], len(ROUNDS[number]))

    sides = [
        (c < 15, (s, c + 1), c > 0),
        (c > 0, (s, c - 1), c < 15),
        (s < 7, (s + 1, c), s > 0),
        (s > 0, (s - 1, c), s < 7),
    ]
    lands = (0, 1, jnp.where(s == 3, 3, 2), jnp.where(s == 5, 2, 3))
    corners = ((2, 3, 0, 4), (3, 4, 7, 3))
    beside = (s + 1 - 2 * (s % 2), c + 1 - 2 * core)
    outer = jnp.logical_or(s % 4 == 0, s % 4 == 3)
    detours = tuple(jnp.logical_and(jnp.logical_and(outer, core == 1 - d), sides[d][0]) for d in range(2))
    held_back = (False, False, s % 4 == 0, s % 4 == 3)
    passes_on = jnp.logical_and(jnp.logical_not(outer), jnp.where(core == 0, c < 14, c > 1))

    small_copies = [
        pltpu.make_async_copy(source, landing, small_sem.at[i])
        for i, (source, landing) in enumerate((
            (border_cols_h, border_cols), (border_rows_h, border_rows), (own_cols_h, own_cols), (volume_h, volume),
        ))
    ]
    small_copies[0].start()
    small_copies[1].start()
    basis_copy = pltpu.make_async_copy(basis_h, basis, basis_sem)
    basis_copy.start()

    def own_copy(step):
        rows = pl.ds(step * UNROLL, UNROLL)
        return pltpu.make_async_copy(own_h.at[rows], own.at[rows], own_sem.at[step])

    barrier = pltpu.get_barrier_semaphore()
    for may_send, target, _ in sides:
        @pl.when(may_send)
        def _():
            pl.semaphore_signal(barrier, inc=1, device_id=target, device_id_type=MESH)
    pl.semaphore_signal(barrier, inc=1, device_id=mate, device_id_type=MESH)

    pl.semaphore_signal(barrier, inc=1, device_id=beside, device_id_type=MESH)
    for step in AROUND:
        pl.semaphore_signal(barrier, inc=1, device_id=ident(moved(chip, *step), core), device_id_type=MESH)

    for copy in small_copies[2:]:
        copy.start()

    for d, (_, _, may_receive) in enumerate(sides):
        @pl.when(jnp.logical_not(may_receive))
        def _():
            recv_rows[d] = jnp.zeros((NB, 128), I32)
            recv_a[d] = jnp.zeros((NB, BS, 2 * BS), BF16)
            recv_b[d] = jnp.zeros((NB, BS, MODES), BF16)

    greeted = sum(jnp.where(may_receive, 1, 0) for _, _, may_receive in sides)
    pl.semaphore_wait(barrier, greeted + 2 + len(AROUND))

    def rows_copy(d, land):
        return pltpu.make_async_remote_copy(
            send_rows.at[d], recv_rows.at[land], rows_ss.at[d], rows_rs.at[land],
            device_id=sides[d][1], device_id_type=MESH,
        )

    def half_copies(d, half, land, count=HALF):
        blocks = pl.ds(half * HALF, count)
        return (
            pltpu.make_async_remote_copy(
                border_h.at[ORDER[d], blocks], recv_a.at[land, blocks], a_ss.at[d, half], a_rs.at[land, half],
                device_id=sides[d][1], device_id_type=MESH,
            ),
            pltpu.make_async_remote_copy(
                send_b.at[d, blocks], recv_b.at[land, blocks], b_ss.at[d, half], b_rs.at[land, half],
                device_id=sides[d][1], device_id_type=MESH,
            ),
        )

    def corner_copies(d, corner, k):
        return (
            pltpu.make_async_remote_copy(
                border_h.at[ORDER[d], HALF + k], relay_a.at[k], in_ss.at[0, k], in_rs.at[0, k],
                device_id=(corner, c), device_id_type=MESH,
            ),
            pltpu.make_async_remote_copy(
                send_b.at[d, HALF + k], relay_b.at[k], in_ss.at[1, k], in_rs.at[1, k],
                device_id=(corner, c), device_id_type=MESH,
            ),
        )

    def side_copies(d, k):
        return (
            pltpu.make_async_remote_copy(
                border_h.at[ORDER[d], NB - DETOUR + k], side_a.at[k], side_ss.at[0, k], side_rs.at[0, k],
                device_id=beside, device_id_type=MESH,
            ),
            pltpu.make_async_remote_copy(
                send_b.at[d, NB - DETOUR + k], side_b.at[k], side_ss.at[1, k], side_rs.at[1, k],
                device_id=beside, device_id_type=MESH,
            ),
        )

    def side_onward_copies(k):
        target = (beside[0], c + 2 - 4 * core)
        return (
            pltpu.make_async_remote_copy(
                side_a.at[k], recv_a.at[core, NB - DETOUR + k], side_out_ss.at[0, k], a_rs.at[core, 1],
                device_id=target, device_id_type=MESH,
            ),
            pltpu.make_async_remote_copy(
                side_b.at[k], recv_b.at[core, NB - DETOUR + k], side_out_ss.at[1, k], b_rs.at[core, 1],
                device_id=target, device_id_type=MESH,
            ),
        )

    def onward_copies(receiver, k):
        return (
            pltpu.make_async_remote_copy(
                relay_a.at[k], recv_a.at[3, HALF + k], out_ss.at[0, k], a_rs.at[3, 1],
                device_id=(receiver, c), device_id_type=MESH,
            ),
            pltpu.make_async_remote_copy(
                relay_b.at[k], recv_b.at[3, HALF + k], out_ss.at[1, k], b_rs.at[3, 1],
                device_id=(receiver, c), device_id_type=MESH,
            ),
        )

    by_corner = {d: (sender, corner) for d, sender, corner, _ in corners}

    def send(d, which):
        if d in by_corner:
            sender, corner = by_corner[d]
            special = s == sender

            @pl.when(special)
            def _():
                for k in range(HALF):
                    corner_copies(d, corner, k)[which].start()
        else:
            special = detours[d]

            @pl.when(special)
            def _():
                for k in range(DETOUR):
                    side_copies(d, k)[which].start()
                half_copies(d, 1, lands[d], HALF - DETOUR)[which].start()

        now = jnp.logical_and(sides[d][0], jnp.logical_not(held_back[d]))

        @pl.when(now)
        def _():
            half_copies(d, 0, lands[d])[which].start()

        @pl.when(jnp.logical_and(now, jnp.logical_not(special)))
        def _():
            half_copies(d, 1, lands[d])[which].start()

    for d in (0, 1, 2, 3):
        send(d, 0)
    small_copies[1].wait()
    for d in range(4):
        for n in range(NB):
            send_rows[d, pl.ds(n, 1), :] = jnp.full((1, 128), border_rows[ORDER[d], n], I32)

        @pl.when(sides[d][0])
        def _():
            rows_copy(d, lands[d]).start()

    small_copies[0].wait()
    basis_copy.wait()
    for d in (0, 1, 2, 3):
        for n in range(NB):
            send_b[d, n] = basis[border_cols[ORDER[d], n]]
        send(d, 1)
    for step in range(STEPS):
        own_copy(step).start()
    tell(0)
    small_copies[2].wait()
    small_copies[3].wait()

    columns = volume[...].T * norm
    for i in range(ROWS // 2):
        volb[2 * i:2 * i + 2] = jnp.broadcast_to(columns[:, i:i + 1], (128, 128)).reshape(2, BS, 128)

    @pl.loop(0, STEPS)
    def _(step):
        own_copy(step).wait()
        for d, _, corner, receiver in corners:
            @pl.when(jnp.logical_and(step >= STEPS - HALF, s == corner))
            def _():
                k = step - (STEPS - HALF)
                for copy in corner_copies(d, corner, k):
                    copy.wait_recv()
                for copy in onward_copies(receiver, k):
                    copy.start()

        @pl.when(step == 2)
        def _():
            told(0)
            tell(1)

        @pl.when(step == 4)
        def _():
            told(1)
            tell(2)

        @pl.when(jnp.logical_and(step == 1, outer))
        def _():
            for d in range(2):
                @pl.when(detours[d])
                def _():
                    for k in range(DETOUR):
                        for copy in side_copies(d, k):
                            copy.wait_send()
            for d in (2, 3):
                @pl.when(held_back[d])
                def _():
                    for half in range(2):
                        for copy in half_copies(d, half, lands[d]):
                            copy.start()

        @pl.when(jnp.logical_and(step >= STEPS - DETOUR, passes_on))
        def _():
            k = step - (STEPS - DETOUR)
            for copy in side_copies(0, k):
                copy.wait_recv()
            for copy in side_onward_copies(k):
                copy.start()

        for j in range(UNROLL):
            i = step * UNROLL + j
            gathered = jnp.concatenate([basis[own_cols[k, i]] for k in range(KOWN)], axis=0)
            sums[i] = lax.dot_general(
                own[i].reshape(KOWN * BS, 2 * BS), gathered, CONTRACT_FIRST, preferred_element_type=F32
            )

    for d, (may_send, _, may_receive) in enumerate(sides):
        @pl.when(may_receive)
        def _():
            rows_copy(d, d).wait_recv()
    targets = recv_rows[...].reshape(SLOTS, 128)
    slot = lax.broadcasted_iota(I32, (SLOTS, 128), 0)
    lane = lax.broadcasted_iota(I32, (SLOTS, 128), 1)
    target_lane = jnp.sum(jnp.where(slot == lane, targets, 0), axis=0, keepdims=True)
    target_lane = jnp.broadcast_to(target_lane, (SLOTS, 128))
    source = jnp.max(jnp.where(targets == lane, ROWS + slot, lane), axis=0, keepdims=True)
    base = jnp.max(
        jnp.where((targets == target_lane) & (slot < lane), ROWS + slot, target_lane), axis=0, keepdims=True
    )
    last = 1 - jnp.max(
        jnp.where((targets == target_lane) & (slot > lane), 1, 0), axis=0, keepdims=True
    )
    table_v[0:1, :] = source
    table_v[1:2, :] = base
    table_v[2:3, :] = last
    table_v[3:4, :] = target_lane[0:1]
    table_v[4:8, :] = jnp.zeros((4, 128), I32)
    table_copy = pltpu.make_async_copy(table_v, table, table_sem)
    table_copy.start()
    table_copy.wait()

    part[...] = jnp.zeros_like(part)

    def add_product(left, right):
        product = lax.dot_general(left, right, CONTRACT_FIRST, preferred_element_type=F32)
        for lanes in range(4):
            part[lanes] += product[:, lanes * 128:(lanes + 1) * 128]

    @pl.loop(0, ROWS // PROJ)
    def _(step):
        for j in range(PROJ):
            i = step * PROJ + j
            keep = jnp.where(table[0, i] == i, 1.0, 0.0).astype(F32)
            scale = volb[i] * keep
            scale = jnp.concatenate([scale, scale], axis=1)
            row = sums[i]
            w_chunk[j, :, 0:MODES] = (row[0:BS] * scale).astype(BF16)
            w_chunk[j, :, MODES:2 * MODES] = (row[BS:2 * BS] * scale).astype(BF16)
        left = basis[pl.ds(step * PROJ, PROJ)].reshape(PROJ * BS, MODES)
        add_product(left, w_chunk[...].reshape(PROJ * BS, 2 * MODES))

    for d in range(4):
        @pl.when(sides[d][2])
        def _():
            for half in range(2):
                for copy in half_copies(d, half, d):
                    copy.wait_recv()

        for n in range(NB):
            m = d * NB + n
            partial = lax.dot_general(recv_a[d, n], recv_b[d, n], CONTRACT_FIRST, preferred_element_type=F32)
            total = sums[table[1, m]] + partial
            sums[ROWS + m] = total
            row = table[3, m]
            scale = volb[row] * table[2, m].astype(F32)
            scale = jnp.concatenate([scale, scale], axis=1)
            w_slot[n, :, 0:MODES] = (total[0:BS] * scale).astype(BF16)
            w_slot[n, :, MODES:2 * MODES] = (total[BS:2 * BS] * scale).astype(BF16)
        left = jnp.concatenate([basis[table[3, d * NB + n]] for n in range(NB)], axis=0)
        add_product(left, w_slot[...].reshape(NB * BS, 2 * MODES))

    told(2)

    for cc in range(2):
        for r in range(2):
            for lanes in range(4):
                for at in range(4):
                    q[cc, pl.ds(at * 128 + lanes * 2 + r, 16, stride=8), :] = part[
                        lanes, pl.ds((at % 2) * 128 + (at // 2) * 4 + 2 * cc + r, 16, stride=8), :
                    ]
    order = [(x + i) % 4 for i in (2, 1, 3, 0)]

    def pair_copy(i):
        tiles = pl.ds(pl.multiple_of(order[i] * 128, 128), 128)
        return pltpu.make_async_remote_copy(
            q.at[1 - core, tiles], pair.at[tiles], pair_ss.at[i], pair_rs.at[i], device_id=mate, device_id_type=MESH
        )

    def sum_copy(i, j):
        from_it = (x - order[i] + 4) % 4 * 16 + (y - j // 4 + 4) % 4 * 4 + (z - j % 4 + 4) % 4
        return from_it, pltpu.make_async_remote_copy(
            h.at[order[i] * 16 + j], recv_h.at[from_it], all_sem.at[0], all_sem.at[1],
            device_id=ident((order[i], j // 4, j % 4), core), device_id_type=MESH,
        )

    for i in range(4):
        pair_copy(i).start()
    for i in range(4):
        pair_copy(i).wait()
        tiles = pl.ds(pl.multiple_of(order[i] * 128, 128), 128)
        h[pl.ds(order[i] * 16, 16)] = (q[core, tiles] + pair[tiles]).reshape(16, 8, 128)

        @pl.loop(0, 16)
        def _(j):
            from_it, copy = sum_copy(i, j)

            @pl.when(from_it != 0)
            def _():
                copy.start()

    @pl.loop(0, ROWS // 4)
    def _(step):
        for j in range(4):
            i = step * 4 + j
            row = sums[table[0, i]]
            applied_out[0, i] = row[0:BS].astype(BF16)
            applied_out[1, i] = row[BS:2 * BS].astype(BF16)

    for d, (may_send, _, _) in enumerate(sides):
        @pl.when(may_send)
        def _():
            rows_copy(d, d).wait_send()
            for copy in half_copies(d, 0, d):
                copy.wait_send()

        special = s == by_corner[d][0] if d in by_corner else detours[d]

        @pl.when(jnp.logical_and(may_send, jnp.logical_not(special)))
        def _():
            for copy in half_copies(d, 1, d):
                copy.wait_send()

        if d not in by_corner:
            @pl.when(special)
            def _():
                for copy in half_copies(d, 1, d, HALF - DETOUR):
                    copy.wait_send()

    @pl.when(passes_on)
    def _():
        for k in range(DETOUR):
            for copy in side_onward_copies(k):
                copy.wait_send()

    for d, sender, corner, receiver in corners:
        @pl.when(s == sender)
        def _():
            for k in range(HALF):
                for copy in corner_copies(d, corner, k):
                    copy.wait_send()

        @pl.when(s == corner)
        def _():
            for k in range(HALF):
                for copy in onward_copies(receiver, k):
                    copy.wait_send()

    pltpu.make_async_remote_copy(
        h.at[pl.ds(1, 63)], recv_h.at[pl.ds(1, 63)], all_sem.at[0], all_sem.at[1], device_id=mate, device_id_type=MESH
    ).wait()
    recv_h[0] = h[x * 16 + y * 4 + z]


PIECES = 4


def write_out(applied, tiles, applied_out, reduced_out, reduced, sems, sem):
    copies = []
    for term in range(2):
        for piece in range(PIECES):
            rows = pl.ds(piece * (ROWS // PIECES), ROWS // PIECES)
            copies.append(pltpu.make_async_copy(applied.at[term, rows], applied_out.at[term, rows], sems.at[term, piece]))
    for copy in copies:
        copy.start()
    mine = tiles[...].reshape(8, 8, 8, 128).sum(axis=1).sum(axis=0)
    for r in range(2):
        for lanes in range(4):
            reduced[r, lanes // 2:lanes // 2 + 1, (lanes % 2) * 128:(lanes % 2 + 1) * 128] = mine[
                lanes * 2 + r:lanes * 2 + r + 1
            ]
    copies.append(pltpu.make_async_copy(reduced, reduced_out, sem))
    copies[-1].start()
    for copy in copies:
        copy.wait()


def local(basis, volume, own_blocks, own_cols, border_blocks, border_cols, border_rows):
    norm = 1.0 / math.sqrt(lax.axis_size("stream") * lax.axis_size("cross") * ROWS * BS)
    vmem = pl.BlockSpec(memory_space=pltpu.VMEM)
    anywhere = pl.BlockSpec(memory_space=pl.ANY)
    dma = pltpu.SemaphoreType.DMA
    applied, tiles = pl.pallas_call(
        functools.partial(kernel, norm),
        name="galerkin",
        in_specs=[anywhere] * 7,
        out_specs=[vmem, vmem],
        out_shape=[
            pltpu.VMEM((2, ROWS, BS, MODES), BF16),
            pltpu.VMEM((64, 8, 128), F32),
        ],
        scratch_shapes=[
            pltpu.SMEM((KOWN, ROWS), I32),
            pltpu.SMEM((4, NB), I32),
            pltpu.SMEM((4, NB), I32),
            pltpu.VMEM((ROWS // 2, 128), F32),
            pltpu.VMEM((ROWS, KOWN, BS, 2 * BS), BF16),
            pltpu.VMEM((ROWS, BS, MODES), BF16),
            pltpu.VMEM((ROWS + SLOTS, 2 * BS, MODES), F32),
            pltpu.VMEM((ROWS, BS, 128), F32),
            pltpu.VMEM((4, NB, 128), I32),
            pltpu.VMEM((4, NB, BS, MODES), BF16),
            pltpu.VMEM((4, NB, 128), I32),
            pltpu.VMEM((4, NB, BS, 2 * BS), BF16),
            pltpu.VMEM((4, NB, BS, MODES), BF16),
            pltpu.VMEM((HALF, BS, 2 * BS), BF16),
            pltpu.VMEM((HALF, BS, MODES), BF16),
            pltpu.VMEM((DETOUR, BS, 2 * BS), BF16),
            pltpu.VMEM((DETOUR, BS, MODES), BF16),
            pltpu.VMEM((8, 128), I32),
            pltpu.SMEM((8, 128), I32),
            pltpu.VMEM((PROJ, BS, 2 * MODES), BF16),
            pltpu.VMEM((NB, BS, 2 * MODES), BF16),
            pltpu.VMEM((4, MODES, 128), F32),
            pltpu.VMEM((2, 512, 128), F32),
            pltpu.VMEM((512, 128), F32),
            pltpu.VMEM((64, 8, 128), F32),
            dma((STEPS,)), dma(()), dma((4,)), dma(()),
            dma((4,)), dma((4,)), dma((4, 2)), dma((4, 2)), dma((4, 2)), dma((4, 2)),
            dma((2, HALF)), dma((2, HALF)), dma((2, HALF)),
            dma((2, DETOUR)), dma((2, DETOUR)), dma((2, DETOUR)),
            dma((4,)), dma((4,)), dma((2,)), pltpu.SemaphoreType.REGULAR((len(ROUNDS),)),
        ],
        compiler_params=pltpu.CompilerParams(
            collective_id=0, has_side_effects=True, vmem_limit_bytes=48 << 20
        ),
        cost_estimate=pl.CostEstimate(flops=4_700_000_000, bytes_accessed=21_000_000, transcendentals=0),
    )(
        own_cols.T,
        border_cols[0],
        border_rows[0],
        basis.reshape(ROWS, BS, MODES),
        volume.reshape(ROWS // 2, 128),
        own_blocks,
        border_blocks[0],
    )
    applied, reduced = pl.pallas_call(
        write_out,
        name="write_out",
        in_specs=[pl.BlockSpec(memory_space=pltpu.VMEM)] * 2,
        out_specs=[anywhere, anywhere],
        out_shape=[
            jax.ShapeDtypeStruct((2, ROWS, BS, MODES), BF16),
            jax.ShapeDtypeStruct((2, 2, MODES), F32),
        ],
        scratch_shapes=[pltpu.VMEM((2, 2, MODES), F32), dma((2, PIECES)), dma(())],
        compiler_params=pltpu.CompilerParams(vmem_limit_bytes=16 << 20),
    )(applied, tiles)
    applied = applied.reshape(2, ROWS * BS, MODES)
    return applied, reduced


def solution(mesh):
    both = ("stream", "cross")
    return jax.shard_map(
        local,
        mesh=mesh,
        in_specs=(
            P(both, None), P(both), P(both, None, None, None), P(both, None),
            P(both, None, None, None, None), P(both, None, None), P(both, None, None),
        ),
        out_specs=(P(None, both, None), P(both, None, None)),
        check_vma=False,
    )
```

```python
import functools
import math

import jax
import jax.numpy as jnp
from jax import lax
from jax.experimental import pallas as pl
from jax.experimental.pallas import tpu as pltpu
from jax.sharding import PartitionSpec as P

MESH = pl.DeviceIdType.MESH
F32, BF16, I32 = jnp.float32, jnp.bfloat16, jnp.int32

ROWS = 96
KOWN = 7
BS = 64
MODES = 256
NB = 8
SLOTS = 4 * NB
UNROLL = 16
STEPS = ROWS // UNROLL
PROJ = 8

CONTRACT_FIRST = (((0,), (0,)), ((), ()))


def ident(chip, core):
    x, y, z = chip
    return ((x % 2) * 4 + y, z * 4 + (x // 2) * 2 + core)


def moved(chip, dx, dy, dz):
    x, y, z = chip
    return ((x + dx) % 4, (y + dy) % 4, (z + dz) % 4)


AROUND = ((1, 0, 0), (3, 0, 0), (0, 1, 0), (0, 3, 0), (0, 0, 1), (0, 0, 3))
ROUNDS = (AROUND, ((2, 0, 0), (0, 2, 0)), ((2, 1, 0), (0, 0, 2)))
ORDER = (2, 3, 0, 1)
HALF = NB // 2
DETOUR = 1


def kernel(
    norm,
    own_cols_h, border_cols_h, border_rows_h, basis_h, volume_h, own_h, border_h,
    applied_out, recv_h,
    own_cols, border_cols, border_rows, volume,
    own, basis, sums, volb, send_rows, send_b, recv_rows, recv_a, recv_b, relay_a, relay_b, side_a, side_b, table_v, table,
    w_chunk, w_slot, part, q, pair, h,
    own_sem, basis_sem, small_sem, table_sem, rows_ss, rows_rs, a_ss, a_rs, b_ss, b_rs,
    in_ss, in_rs, out_ss, side_ss, side_rs, side_out_ss, pair_ss, pair_rs, all_sem, known,
):
    s, c = lax.axis_index("stream"), lax.axis_index("cross")
    x, y, z = chip = ((c // 2) % 2 * 2 + s // 4, s % 4, c // 4)
    core = c % 2
    mate = ident(chip, 1 - core)

    def tell(number):
        for step in ROUNDS[number]:
            pl.semaphore_signal(known.at[number], inc=1, device_id=ident(moved(chip, *step), core), device_id_type=MESH)

    def told(number):
        pl.semaphore_wait(known.at[number], len(ROUNDS[number]))

    sides = [
        (c < 15, (s, c + 1), c > 0),
        (c > 0, (s, c - 1), c < 15),
        (s < 7, (s + 1, c), s > 0),
        (s > 0, (s - 1, c), s < 7),
    ]
    lands = (0, 1, jnp.where(s == 3, 3, 2), jnp.where(s == 5, 2, 3))
    corners = ((2, 3, 0, 4), (3, 4, 7, 3))
    beside = (s + 1 - 2 * (s % 2), c + 1 - 2 * core)
    outer = jnp.logical_or(s % 4 == 0, s % 4 == 3)
    detours = tuple(jnp.logical_and(jnp.logical_and(outer, core == 1 - d), sides[d][0]) for d in range(2))
    held_back = (False, False, s % 4 == 0, s % 4 == 3)
    passes_on = jnp.logical_and(jnp.logical_not(outer), jnp.where(core == 0, c < 14, c > 1))

    small_copies = [
        pltpu.make_async_copy(source, landing, small_sem.at[i])
        for i, (source, landing) in enumerate((
            (border_cols_h, border_cols), (border_rows_h, border_rows), (own_cols_h, own_cols), (volume_h, volume),
        ))
    ]
    small_copies[0].start()
    small_copies[1].start()
    basis_copy = pltpu.make_async_copy(basis_h, basis, basis_sem)
    basis_copy.start()

    def own_copy(step):
        rows = pl.ds(step * UNROLL, UNROLL)
        return pltpu.make_async_copy(own_h.at[rows], own.at[rows], own_sem.at[step])

    barrier = pltpu.get_barrier_semaphore()
    for may_send, target, _ in sides:
        @pl.when(may_send)
        def _():
            pl.semaphore_signal(barrier, inc=1, device_id=target, device_id_type=MESH)
    pl.semaphore_signal(barrier, inc=1, device_id=mate, device_id_type=MESH)

    pl.semaphore_signal(barrier, inc=1, device_id=beside, device_id_type=MESH)
    for step in AROUND:
        pl.semaphore_signal(barrier, inc=1, device_id=ident(moved(chip, *step), core), device_id_type=MESH)

    for copy in small_copies[2:]:
        copy.start()

    for d, (_, _, may_receive) in enumerate(sides):
        @pl.when(jnp.logical_not(may_receive))
        def _():
            recv_rows[d] = jnp.zeros((NB, 128), I32)
            recv_a[d] = jnp.zeros((NB, BS, 2 * BS), BF16)
            recv_b[d] = jnp.zeros((NB, BS, MODES), BF16)

    greeted = sum(jnp.where(may_receive, 1, 0) for _, _, may_receive in sides)
    pl.semaphore_wait(barrier, greeted + 2 + len(AROUND))

    def rows_copy(d, land):
        return pltpu.make_async_remote_copy(
            send_rows.at[d], recv_rows.at[land], rows_ss.at[d], rows_rs.at[land],
            device_id=sides[d][1], device_id_type=MESH,
        )

    def half_copies(d, half, land, count=HALF):
        blocks = pl.ds(half * HALF, count)
        return (
            pltpu.make_async_remote_copy(
                border_h.at[ORDER[d], blocks], recv_a.at[land, blocks], a_ss.at[d, half], a_rs.at[land, half],
                device_id=sides[d][1], device_id_type=MESH,
            ),
            pltpu.make_async_remote_copy(
                send_b.at[d, blocks], recv_b.at[land, blocks], b_ss.at[d, half], b_rs.at[land, half],
                device_id=sides[d][1], device_id_type=MESH,
            ),
        )

    def corner_copies(d, corner, k):
        return (
            pltpu.make_async_remote_copy(
                border_h.at[ORDER[d], HALF + k], relay_a.at[k], in_ss.at[0, k], in_rs.at[0, k],
                device_id=(corner, c), device_id_type=MESH,
            ),
            pltpu.make_async_remote_copy(
                send_b.at[d, HALF + k], relay_b.at[k], in_ss.at[1, k], in_rs.at[1, k],
                device_id=(corner, c), device_id_type=MESH,
            ),
        )

    def side_copies(d, k):
        return (
            pltpu.make_async_remote_copy(
                border_h.at[ORDER[d], NB - DETOUR + k], side_a.at[k], side_ss.at[0, k], side_rs.at[0, k],
                device_id=beside, device_id_type=MESH,
            ),
            pltpu.make_async_remote_copy(
                send_b.at[d, NB - DETOUR + k], side_b.at[k], side_ss.at[1, k], side_rs.at[1, k],
                device_id=beside, device_id_type=MESH,
            ),
        )

    def side_onward_copies(k):
        target = (beside[0], c + 2 - 4 * core)
        return (
            pltpu.make_async_remote_copy(
                side_a.at[k], recv_a.at[core, NB - DETOUR + k], side_out_ss.at[0, k], a_rs.at[core, 1],
                device_id=target, device_id_type=MESH,
            ),
            pltpu.make_async_remote_copy(
                side_b.at[k], recv_b.at[core, NB - DETOUR + k], side_out_ss.at[1, k], b_rs.at[core, 1],
                device_id=target, device_id_type=MESH,
            ),
        )

    def onward_copies(receiver, k):
        return (
            pltpu.make_async_remote_copy(
                relay_a.at[k], recv_a.at[3, HALF + k], out_ss.at[0, k], a_rs.at[3, 1],
                device_id=(receiver, c), device_id_type=MESH,
            ),
            pltpu.make_async_remote_copy(
                relay_b.at[k], recv_b.at[3, HALF + k], out_ss.at[1, k], b_rs.at[3, 1],
                device_id=(receiver, c), device_id_type=MESH,
            ),
        )

    by_corner = {d: (sender, corner) for d, sender, corner, _ in corners}

    def send(d, which):
        if d in by_corner:
            sender, corner = by_corner[d]
            special = s == sender

            @pl.when(special)
            def _():
                for k in range(HALF):
                    corner_copies(d, corner, k)[which].start()
        else:
            special = detours[d]

            @pl.when(special)
            def _():
                for k in range(DETOUR):
                    side_copies(d, k)[which].start()
                half_copies(d, 1, lands[d], HALF - DETOUR)[which].start()

        now = jnp.logical_and(sides[d][0], jnp.logical_not(held_back[d]))

        @pl.when(now)
        def _():
            half_copies(d, 0, lands[d])[which].start()

        @pl.when(jnp.logical_and(now, jnp.logical_not(special)))
        def _():
            half_copies(d, 1, lands[d])[which].start()

    for d in (0, 1, 2, 3):
        send(d, 0)
    small_copies[1].wait()
    for d in range(4):
        for n in range(NB):
            send_rows[d, pl.ds(n, 1), :] = jnp.full((1, 128), border_rows[ORDER[d], n], I32)

        @pl.when(sides[d][0])
        def _():
            rows_copy(d, lands[d]).start()

    small_copies[0].wait()
    basis_copy.wait()
    for d in (0, 1, 2, 3):
        for n in range(NB):
            send_b[d, n] = basis[border_cols[ORDER[d], n]]
        send(d, 1)
    for step in range(STEPS):
        own_copy(step).start()
    tell(0)
    small_copies[2].wait()
    small_copies[3].wait()

    columns = volume[...].T * norm
    for i in range(ROWS // 2):
        volb[2 * i:2 * i + 2] = jnp.broadcast_to(columns[:, i:i + 1], (128, 128)).reshape(2, BS, 128)

    @pl.loop(0, STEPS)
    def _(step):
        own_copy(step).wait()
        for d, _, corner, receiver in corners:
            @pl.when(jnp.logical_and(step >= STEPS - HALF, s == corner))
            def _():
                k = step - (STEPS - HALF)
                for copy in corner_copies(d, corner, k):
                    copy.wait_recv()
                for copy in onward_copies(receiver, k):
                    copy.start()

        @pl.when(step == 2)
        def _():
            told(0)
            tell(1)

        @pl.when(step == 4)
        def _():
            told(1)
            tell(2)

        @pl.when(jnp.logical_and(step == 1, outer))
        def _():
            for d in range(2):
                @pl.when(detours[d])
                def _():
                    for k in range(DETOUR):
                        for copy in side_copies(d, k):
                            copy.wait_send()
            for d in (2, 3):
                @pl.when(held_back[d])
                def _():
                    for half in range(2):
                        for copy in half_copies(d, half, lands[d]):
                            copy.start()

        @pl.when(jnp.logical_and(step >= STEPS - DETOUR, passes_on))
        def _():
            k = step - (STEPS - DETOUR)
            for copy in side_copies(0, k):
                copy.wait_recv()
            for copy in side_onward_copies(k):
                copy.start()

        for j in range(UNROLL):
            i = step * UNROLL + j
            gathered = jnp.concatenate([basis[own_cols[k, i]] for k in range(KOWN)], axis=0)
            sums[i] = lax.dot_general(
                own[i].reshape(KOWN * BS, 2 * BS), gathered, CONTRACT_FIRST, preferred_element_type=F32
            )

    for d, (may_send, _, may_receive) in enumerate(sides):
        @pl.when(may_receive)
        def _():
            rows_copy(d, d).wait_recv()
    targets = recv_rows[...].reshape(SLOTS, 128)
    slot = lax.broadcasted_iota(I32, (SLOTS, 128), 0)
    lane = lax.broadcasted_iota(I32, (SLOTS, 128), 1)
    target_lane = jnp.sum(jnp.where(slot == lane, targets, 0), axis=0, keepdims=True)
    target_lane = jnp.broadcast_to(target_lane, (SLOTS, 128))
    source = jnp.max(jnp.where(targets == lane, ROWS + slot, lane), axis=0, keepdims=True)
    base = jnp.max(
        jnp.where((targets == target_lane) & (slot < lane), ROWS + slot, target_lane), axis=0, keepdims=True
    )
    last = 1 - jnp.max(
        jnp.where((targets == target_lane) & (slot > lane), 1, 0), axis=0, keepdims=True
    )
    table_v[0:1, :] = source
    table_v[1:2, :] = base
    table_v[2:3, :] = last
    table_v[3:4, :] = target_lane[0:1]
    table_v[4:8, :] = jnp.zeros((4, 128), I32)
    table_copy = pltpu.make_async_copy(table_v, table, table_sem)
    table_copy.start()
    table_copy.wait()

    part[...] = jnp.zeros_like(part)

    def add_product(left, right):
        product = lax.dot_general(left, right, CONTRACT_FIRST, preferred_element_type=F32)
        for lanes in range(4):
            part[lanes] += product[:, lanes * 128:(lanes + 1) * 128]

    @pl.loop(0, ROWS // PROJ)
    def _(step):
        for j in range(PROJ):
            i = step * PROJ + j
            keep = jnp.where(table[0, i] == i, 1.0, 0.0).astype(F32)
            scale = volb[i] * keep
            scale = jnp.concatenate([scale, scale], axis=1)
            row = sums[i]
            w_chunk[j, :, 0:MODES] = (row[0:BS] * scale).astype(BF16)
            w_chunk[j, :, MODES:2 * MODES] = (row[BS:2 * BS] * scale).astype(BF16)
        left = basis[pl.ds(step * PROJ, PROJ)].reshape(PROJ * BS, MODES)
        add_product(left, w_chunk[...].reshape(PROJ * BS, 2 * MODES))

    for d in range(4):
        @pl.when(sides[d][2])
        def _():
            for half in range(2):
                for copy in half_copies(d, half, d):
                    copy.wait_recv()

        for n in range(NB):
            m = d * NB + n
            partial = lax.dot_general(recv_a[d, n], recv_b[d, n], CONTRACT_FIRST, preferred_element_type=F32)
            total = sums[table[1, m]] + partial
            sums[ROWS + m] = total
            row = table[3, m]
            scale = volb[row] * table[2, m].astype(F32)
            scale = jnp.concatenate([scale, scale], axis=1)
            w_slot[n, :, 0:MODES] = (total[0:BS] * scale).astype(BF16)
            w_slot[n, :, MODES:2 * MODES] = (total[BS:2 * BS] * scale).astype(BF16)
        left = jnp.concatenate([basis[table[3, d * NB + n]] for n in range(NB)], axis=0)
        add_product(left, w_slot[...].reshape(NB * BS, 2 * MODES))

    told(2)

    for cc in range(2):
        for r in range(2):
            for lanes in range(4):
                for at in range(4):
                    q[cc, pl.ds(at * 128 + lanes * 2 + r, 16, stride=8), :] = part[
                        lanes, pl.ds((at % 2) * 128 + (at // 2) * 4 + 2 * cc + r, 16, stride=8), :
                    ]
    def pair_copy(i):
        tiles = pl.ds(i * 128, 128)
        return pltpu.make_async_remote_copy(
            q.at[1 - core, tiles], pair.at[tiles], pair_ss.at[i], pair_rs.at[i], device_id=mate, device_id_type=MESH
        )

    for i in range(4):
        pair_copy(i).start()
    for i in range(4):
        pair_copy(i).wait()
        tiles = pl.ds(i * 128, 128)
        h[pl.ds(i * 16, 16)] = (q[core, tiles] + pair[tiles]).reshape(16, 8, 128)

    @pl.loop(0, 64)
    def _(k):
        to = (k // 4 % 4, k % 4, k // 16)
        from_it = (x - to[0] + 4) % 4 * 16 + (y - to[1] + 4) % 4 * 4 + (z - to[2] + 4) % 4

        @pl.when(from_it != 0)
        def _():
            pltpu.make_async_remote_copy(
                h.at[to[0] * 16 + to[1] * 4 + to[2]], recv_h.at[from_it], all_sem.at[0], all_sem.at[1],
                device_id=ident(to, core), device_id_type=MESH,
            ).start()

    @pl.loop(0, ROWS // 4)
    def _(step):
        for j in range(4):
            i = step * 4 + j
            row = sums[table[0, i]]
            applied_out[0, i] = row[0:BS].astype(BF16)
            applied_out[1, i] = row[BS:2 * BS].astype(BF16)

    for d, (may_send, _, _) in enumerate(sides):
        @pl.when(may_send)
        def _():
            rows_copy(d, d).wait_send()
            for copy in half_copies(d, 0, d):
                copy.wait_send()

        special = s == by_corner[d][0] if d in by_corner else detours[d]

        @pl.when(jnp.logical_and(may_send, jnp.logical_not(special)))
        def _():
            for copy in half_copies(d, 1, d):
                copy.wait_send()

        if d not in by_corner:
            @pl.when(special)
            def _():
                for copy in half_copies(d, 1, d, HALF - DETOUR):
                    copy.wait_send()

    @pl.when(passes_on)
    def _():
        for k in range(DETOUR):
            for copy in side_onward_copies(k):
                copy.wait_send()

    for d, sender, corner, receiver in corners:
        @pl.when(s == sender)
        def _():
            for k in range(HALF):
                for copy in corner_copies(d, corner, k):
                    copy.wait_send()

        @pl.when(s == corner)
        def _():
            for k in range(HALF):
                for copy in onward_copies(receiver, k):
                    copy.wait_send()

    pltpu.make_async_remote_copy(
        h.at[pl.ds(1, 63)], recv_h.at[pl.ds(1, 63)], all_sem.at[0], all_sem.at[1], device_id=mate, device_id_type=MESH
    ).wait()
    recv_h[0] = h[x * 16 + y * 4 + z]


PIECES = 4


def write_out(applied, tiles, applied_out, reduced_out, reduced, sems, sem):
    copies = []
    for term in range(2):
        for piece in range(PIECES):
            rows = pl.ds(piece * (ROWS // PIECES), ROWS // PIECES)
            copies.append(pltpu.make_async_copy(applied.at[term, rows], applied_out.at[term, rows], sems.at[term, piece]))
    for copy in copies:
        copy.start()
    mine = tiles[...].reshape(8, 8, 8, 128).sum(axis=1).sum(axis=0)
    for r in range(2):
        for lanes in range(4):
            reduced[r, lanes // 2:lanes // 2 + 1, (lanes % 2) * 128:(lanes % 2 + 1) * 128] = mine[
                lanes * 2 + r:lanes * 2 + r + 1
            ]
    copies.append(pltpu.make_async_copy(reduced, reduced_out, sem))
    copies[-1].start()
    for copy in copies:
        copy.wait()


def local(basis, volume, own_blocks, own_cols, border_blocks, border_cols, border_rows):
    norm = 1.0 / math.sqrt(lax.axis_size("stream") * lax.axis_size("cross") * ROWS * BS)
    vmem = pl.BlockSpec(memory_space=pltpu.VMEM)
    anywhere = pl.BlockSpec(memory_space=pl.ANY)
    dma = pltpu.SemaphoreType.DMA
    applied, tiles = pl.pallas_call(
        functools.partial(kernel, norm),
        name="galerkin",
        in_specs=[anywhere] * 7,
        out_specs=[vmem, vmem],
        out_shape=[
            pltpu.VMEM((2, ROWS, BS, MODES), BF16),
            pltpu.VMEM((64, 8, 128), F32),
        ],
        scratch_shapes=[
            pltpu.SMEM((KOWN, ROWS), I32),
            pltpu.SMEM((4, NB), I32),
            pltpu.SMEM((4, NB), I32),
            pltpu.VMEM((ROWS // 2, 128), F32),
            pltpu.VMEM((ROWS, KOWN, BS, 2 * BS), BF16),
            pltpu.VMEM((ROWS, BS, MODES), BF16),
            pltpu.VMEM((ROWS + SLOTS, 2 * BS, MODES), F32),
            pltpu.VMEM((ROWS, BS, 128), F32),
            pltpu.VMEM((4, NB, 128), I32),
            pltpu.VMEM((4, NB, BS, MODES), BF16),
            pltpu.VMEM((4, NB, 128), I32),
            pltpu.VMEM((4, NB, BS, 2 * BS), BF16),
            pltpu.VMEM((4, NB, BS, MODES), BF16),
            pltpu.VMEM((HALF, BS, 2 * BS), BF16),
            pltpu.VMEM((HALF, BS, MODES), BF16),
            pltpu.VMEM((DETOUR, BS, 2 * BS), BF16),
            pltpu.VMEM((DETOUR, BS, MODES), BF16),
            pltpu.VMEM((8, 128), I32),
            pltpu.SMEM((8, 128), I32),
            pltpu.VMEM((PROJ, BS, 2 * MODES), BF16),
            pltpu.VMEM((NB, BS, 2 * MODES), BF16),
            pltpu.VMEM((4, MODES, 128), F32),
            pltpu.VMEM((2, 512, 128), F32),
            pltpu.VMEM((512, 128), F32),
            pltpu.VMEM((64, 8, 128), F32),
            dma((STEPS,)), dma(()), dma((4,)), dma(()),
            dma((4,)), dma((4,)), dma((4, 2)), dma((4, 2)), dma((4, 2)), dma((4, 2)),
            dma((2, HALF)), dma((2, HALF)), dma((2, HALF)),
            dma((2, DETOUR)), dma((2, DETOUR)), dma((2, DETOUR)),
            dma((4,)), dma((4,)), dma((2,)), pltpu.SemaphoreType.REGULAR((len(ROUNDS),)),
        ],
        compiler_params=pltpu.CompilerParams(
            collective_id=0, has_side_effects=True, vmem_limit_bytes=48 << 20
        ),
        cost_estimate=pl.CostEstimate(flops=4_700_000_000, bytes_accessed=21_000_000, transcendentals=0),
    )(
        own_cols.T,
        border_cols[0],
        border_rows[0],
        basis.reshape(ROWS, BS, MODES),
        volume.reshape(ROWS // 2, 128),
        own_blocks,
        border_blocks[0],
    )
    applied, reduced = pl.pallas_call(
        write_out,
        name="write_out",
        in_specs=[pl.BlockSpec(memory_space=pltpu.VMEM)] * 2,
        out_specs=[anywhere, anywhere],
        out_shape=[
            jax.ShapeDtypeStruct((2, ROWS, BS, MODES), BF16),
            jax.ShapeDtypeStruct((2, 2, MODES), F32),
        ],
        scratch_shapes=[pltpu.VMEM((2, 2, MODES), F32), dma((2, PIECES)), dma(())],
        compiler_params=pltpu.CompilerParams(vmem_limit_bytes=16 << 20),
    )(applied, tiles)
    applied = applied.reshape(2, ROWS * BS, MODES)
    return applied, reduced


def solution(mesh):
    both = ("stream", "cross")
    return jax.shard_map(
        local,
        mesh=mesh,
        in_specs=(
            P(both, None), P(both), P(both, None, None, None), P(both, None),
            P(both, None, None, None, None), P(both, None, None), P(both, None, None),
        ),
        out_specs=(P(None, both, None), P(both, None, None)),
        check_vma=False,
    )
```

```python
import functools
import math

import jax
import jax.numpy as jnp
from jax import lax
from jax.experimental import pallas as pl
from jax.experimental.pallas import tpu as pltpu
from jax.sharding import PartitionSpec as P

MESH = pl.DeviceIdType.MESH
F32, BF16, I32 = jnp.float32, jnp.bfloat16, jnp.int32

ROWS = 96
KOWN = 7
BS = 64
MODES = 256
NB = 8
SLOTS = 4 * NB
UNROLL = 16
STEPS = ROWS // UNROLL
PROJ = 8

CONTRACT_FIRST = (((0,), (0,)), ((), ()))


def ident(chip, core):
    x, y, z = chip
    return ((x % 2) * 4 + y, z * 4 + (x // 2) * 2 + core)


def moved(chip, dx, dy, dz):
    x, y, z = chip
    return ((x + dx) % 4, (y + dy) % 4, (z + dz) % 4)


AROUND = ((1, 0, 0), (3, 0, 0), (0, 1, 0), (0, 3, 0), (0, 0, 1), (0, 0, 3))
ROUNDS = (AROUND, ((2, 0, 0), (0, 2, 0)), ((2, 1, 0), (0, 0, 2)))
ORDER = (2, 3, 0, 1)
HALF = NB // 2
DETOUR = 1


def kernel(
    norm,
    own_cols_h, border_cols_h, border_rows_h, basis_h, volume_h, own_h, border_h,
    applied_out, recv_h,
    own_cols, border_cols, border_rows, volume,
    own, basis, sums, volb, send_rows, send_b, recv_rows, recv_a, recv_b, relay_a, relay_b, side_a, side_b, table_v, table,
    w_chunk, w_slot, part, q, pair, h,
    own_sem, basis_sem, small_sem, table_sem, rows_ss, rows_rs, a_ss, a_rs, b_ss, b_rs,
    in_ss, in_rs, out_ss, side_ss, side_rs, side_out_ss, pair_ss, pair_rs, all_sem, known,
):
    s, c = lax.axis_index("stream"), lax.axis_index("cross")
    x, y, z = chip = ((c // 2) % 2 * 2 + s // 4, s % 4, c // 4)
    core = c % 2
    mate = ident(chip, 1 - core)

    def tell(number):
        for step in ROUNDS[number]:
            pl.semaphore_signal(known.at[number], inc=1, device_id=ident(moved(chip, *step), core), device_id_type=MESH)

    def told(number):
        pl.semaphore_wait(known.at[number], len(ROUNDS[number]))

    sides = [
        (c < 15, (s, c + 1), c > 0),
        (c > 0, (s, c - 1), c < 15),
        (s < 7, (s + 1, c), s > 0),
        (s > 0, (s - 1, c), s < 7),
    ]
    lands = (0, 1, jnp.where(s == 3, 3, 2), jnp.where(s == 5, 2, 3))
    corners = ((2, 3, 0, 4), (3, 4, 7, 3))
    beside = (s + 1 - 2 * (s % 2), c + 1 - 2 * core)
    outer = jnp.logical_or(s % 4 == 0, s % 4 == 3)
    detours = tuple(jnp.logical_and(jnp.logical_and(outer, core == 1 - d), sides[d][0]) for d in range(2))
    held_back = (False, False, s % 4 == 0, s % 4 == 3)
    passes_on = jnp.logical_and(jnp.logical_not(outer), jnp.where(core == 0, c < 14, c > 1))

    small_copies = [
        pltpu.make_async_copy(source, landing, small_sem.at[i])
        for i, (source, landing) in enumerate((
            (border_cols_h, border_cols), (border_rows_h, border_rows), (own_cols_h, own_cols), (volume_h, volume),
        ))
    ]
    small_copies[0].start()
    small_copies[1].start()
    basis_copy = pltpu.make_async_copy(basis_h, basis, basis_sem)
    basis_copy.start()

    def own_copy(step):
        rows = pl.ds(step * UNROLL, UNROLL)
        return pltpu.make_async_copy(own_h.at[rows], own.at[rows], own_sem.at[step])

    barrier = pltpu.get_barrier_semaphore()
    for may_send, target, _ in sides:
        @pl.when(may_send)
        def _():
            pl.semaphore_signal(barrier, inc=1, device_id=target, device_id_type=MESH)
    pl.semaphore_signal(barrier, inc=1, device_id=mate, device_id_type=MESH)

    pl.semaphore_signal(barrier, inc=1, device_id=beside, device_id_type=MESH)
    for step in AROUND:
        pl.semaphore_signal(barrier, inc=1, device_id=ident(moved(chip, *step), core), device_id_type=MESH)

    for copy in small_copies[2:]:
        copy.start()

    for d, (_, _, may_receive) in enumerate(sides):
        @pl.when(jnp.logical_not(may_receive))
        def _():
            recv_rows[d] = jnp.zeros((NB, 128), I32)
            recv_a[d] = jnp.zeros((NB, BS, 2 * BS), BF16)
            recv_b[d] = jnp.zeros((NB, BS, MODES), BF16)

    greeted = sum(jnp.where(may_receive, 1, 0) for _, _, may_receive in sides)
    pl.semaphore_wait(barrier, greeted + 2 + len(AROUND))

    def rows_copy(d, land):
        return pltpu.make_async_remote_copy(
            send_rows.at[d], recv_rows.at[land], rows_ss.at[d], rows_rs.at[land],
            device_id=sides[d][1], device_id_type=MESH,
        )

    def half_copies(d, half, land, count=HALF):
        blocks = pl.ds(half * HALF, count)
        return (
            pltpu.make_async_remote_copy(
                border_h.at[ORDER[d], blocks], recv_a.at[land, blocks], a_ss.at[d, half], a_rs.at[land, half],
                device_id=sides[d][1], device_id_type=MESH,
            ),
            pltpu.make_async_remote_copy(
                send_b.at[d, blocks], recv_b.at[land, blocks], b_ss.at[d, half], b_rs.at[land, half],
                device_id=sides[d][1], device_id_type=MESH,
            ),
        )

    def corner_copies(d, corner, k):
        return (
            pltpu.make_async_remote_copy(
                border_h.at[ORDER[d], HALF + k], relay_a.at[k], in_ss.at[0, k], in_rs.at[0, k],
                device_id=(corner, c), device_id_type=MESH,
            ),
            pltpu.make_async_remote_copy(
                send_b.at[d, HALF + k], relay_b.at[k], in_ss.at[1, k], in_rs.at[1, k],
                device_id=(corner, c), device_id_type=MESH,
            ),
        )

    def side_copies(d, k):
        return (
            pltpu.make_async_remote_copy(
                border_h.at[ORDER[d], NB - DETOUR + k], side_a.at[k], side_ss.at[0, k], side_rs.at[0, k],
                device_id=beside, device_id_type=MESH,
            ),
            pltpu.make_async_remote_copy(
                send_b.at[d, NB - DETOUR + k], side_b.at[k], side_ss.at[1, k], side_rs.at[1, k],
                device_id=beside, device_id_type=MESH,
            ),
        )

    def side_onward_copies(k):
        target = (beside[0], c + 2 - 4 * core)
        return (
            pltpu.make_async_remote_copy(
                side_a.at[k], recv_a.at[core, NB - DETOUR + k], side_out_ss.at[0, k], a_rs.at[core, 1],
                device_id=target, device_id_type=MESH,
            ),
            pltpu.make_async_remote_copy(
                side_b.at[k], recv_b.at[core, NB - DETOUR + k], side_out_ss.at[1, k], b_rs.at[core, 1],
                device_id=target, device_id_type=MESH,
            ),
        )

    def onward_copies(receiver, k):
        return (
            pltpu.make_async_remote_copy(
                relay_a.at[k], recv_a.at[3, HALF + k], out_ss.at[0, k], a_rs.at[3, 1],
                device_id=(receiver, c), device_id_type=MESH,
            ),
            pltpu.make_async_remote_copy(
                relay_b.at[k], recv_b.at[3, HALF + k], out_ss.at[1, k], b_rs.at[3, 1],
                device_id=(receiver, c), device_id_type=MESH,
            ),
        )

    by_corner = {d: (sender, corner) for d, sender, corner, _ in corners}

    def send(d, which):
        if d in by_corner:
            sender, corner = by_corner[d]
            special = s == sender

            @pl.when(special)
            def _():
                for k in range(HALF):
                    corner_copies(d, corner, k)[which].start()
        else:
            special = detours[d]

            @pl.when(special)
            def _():
                for k in range(DETOUR):
                    side_copies(d, k)[which].start()
                half_copies(d, 1, lands[d], HALF - DETOUR)[which].start()

        now = jnp.logical_and(sides[d][0], jnp.logical_not(held_back[d]))

        @pl.when(now)
        def _():
            half_copies(d, 0, lands[d])[which].start()

        @pl.when(jnp.logical_and(now, jnp.logical_not(special)))
        def _():
            half_copies(d, 1, lands[d])[which].start()

    for d in (0, 1, 2, 3):
        send(d, 0)
    small_copies[1].wait()
    for d in range(4):
        for n in range(NB):
            send_rows[d, pl.ds(n, 1), :] = jnp.full((1, 128), border_rows[ORDER[d], n], I32)

        @pl.when(sides[d][0])
        def _():
            rows_copy(d, lands[d]).start()

    small_copies[0].wait()
    basis_copy.wait()
    for d in (0, 1, 2, 3):
        for n in range(NB):
            send_b[d, n] = basis[border_cols[ORDER[d], n]]
        send(d, 1)
    for step in range(STEPS):
        own_copy(step).start()
    tell(0)
    small_copies[2].wait()
    small_copies[3].wait()

    columns = volume[...].T * norm
    for i in range(ROWS // 2):
        volb[2 * i:2 * i + 2] = jnp.broadcast_to(columns[:, i:i + 1], (128, 128)).reshape(2, BS, 128)

    @pl.loop(0, STEPS)
    def _(step):
        own_copy(step).wait()
        for d, _, corner, receiver in corners:
            @pl.when(jnp.logical_and(step >= STEPS - HALF, s == corner))
            def _():
                k = step - (STEPS - HALF)
                for copy in corner_copies(d, corner, k):
                    copy.wait_recv()
                for copy in onward_copies(receiver, k):
                    copy.start()

        @pl.when(step == 2)
        def _():
            told(0)
            tell(1)

        @pl.when(step == 4)
        def _():
            told(1)
            tell(2)

        @pl.when(jnp.logical_and(step == 0, outer))
        def _():
            for d in range(2):
                @pl.when(detours[d])
                def _():
                    for k in range(DETOUR):
                        for copy in side_copies(d, k):
                            copy.wait_send()
            for d in (2, 3):
                @pl.when(held_back[d])
                def _():
                    for half in range(2):
                        for copy in half_copies(d, half, lands[d]):
                            copy.start()

        @pl.when(jnp.logical_and(step >= STEPS - DETOUR, passes_on))
        def _():
            k = step - (STEPS - DETOUR)
            for copy in side_copies(0, k):
                copy.wait_recv()
            for copy in side_onward_copies(k):
                copy.start()

        for j in range(UNROLL):
            i = step * UNROLL + j
            gathered = jnp.concatenate([basis[own_cols[k, i]] for k in range(KOWN)], axis=0)
            sums[i] = lax.dot_general(
                own[i].reshape(KOWN * BS, 2 * BS), gathered, CONTRACT_FIRST, preferred_element_type=F32
            )

    for d, (may_send, _, may_receive) in enumerate(sides):
        @pl.when(may_receive)
        def _():
            rows_copy(d, d).wait_recv()
    targets = recv_rows[...].reshape(SLOTS, 128)
    slot = lax.broadcasted_iota(I32, (SLOTS, 128), 0)
    lane = lax.broadcasted_iota(I32, (SLOTS, 128), 1)
    target_lane = jnp.sum(jnp.where(slot == lane, targets, 0), axis=0, keepdims=True)
    target_lane = jnp.broadcast_to(target_lane, (SLOTS, 128))
    source = jnp.max(jnp.where(targets == lane, ROWS + slot, lane), axis=0, keepdims=True)
    base = jnp.max(
        jnp.where((targets == target_lane) & (slot < lane), ROWS + slot, target_lane), axis=0, keepdims=True
    )
    last = 1 - jnp.max(
        jnp.where((targets == target_lane) & (slot > lane), 1, 0), axis=0, keepdims=True
    )
    table_v[0:1, :] = source
    table_v[1:2, :] = base
    table_v[2:3, :] = last
    table_v[3:4, :] = target_lane[0:1]
    table_v[4:8, :] = jnp.zeros((4, 128), I32)
    table_copy = pltpu.make_async_copy(table_v, table, table_sem)
    table_copy.start()
    table_copy.wait()

    part[...] = jnp.zeros_like(part)

    def add_product(left, right):
        product = lax.dot_general(left, right, CONTRACT_FIRST, preferred_element_type=F32)
        for lanes in range(4):
            part[lanes] += product[:, lanes * 128:(lanes + 1) * 128]

    @pl.loop(0, ROWS // PROJ)
    def _(step):
        for j in range(PROJ):
            i = step * PROJ + j
            keep = jnp.where(table[0, i] == i, 1.0, 0.0).astype(F32)
            scale = volb[i] * keep
            scale = jnp.concatenate([scale, scale], axis=1)
            row = sums[i]
            w_chunk[j, :, 0:MODES] = (row[0:BS] * scale).astype(BF16)
            w_chunk[j, :, MODES:2 * MODES] = (row[BS:2 * BS] * scale).astype(BF16)
        left = basis[pl.ds(step * PROJ, PROJ)].reshape(PROJ * BS, MODES)
        add_product(left, w_chunk[...].reshape(PROJ * BS, 2 * MODES))

    for d in range(4):
        @pl.when(sides[d][2])
        def _():
            for half in range(2):
                for copy in half_copies(d, half, d):
                    copy.wait_recv()

        for n in range(NB):
            m = d * NB + n
            partial = lax.dot_general(recv_a[d, n], recv_b[d, n], CONTRACT_FIRST, preferred_element_type=F32)
            total = sums[table[1, m]] + partial
            sums[ROWS + m] = total
            row = table[3, m]
            scale = volb[row] * table[2, m].astype(F32)
            scale = jnp.concatenate([scale, scale], axis=1)
            w_slot[n, :, 0:MODES] = (total[0:BS] * scale).astype(BF16)
            w_slot[n, :, MODES:2 * MODES] = (total[BS:2 * BS] * scale).astype(BF16)
        left = jnp.concatenate([basis[table[3, d * NB + n]] for n in range(NB)], axis=0)
        add_product(left, w_slot[...].reshape(NB * BS, 2 * MODES))

    told(2)

    for cc in range(2):
        for r in range(2):
            for lanes in range(4):
                for at in range(4):
                    q[cc, pl.ds(at * 128 + lanes * 2 + r, 16, stride=8), :] = part[
                        lanes, pl.ds((at % 2) * 128 + (at // 2) * 4 + 2 * cc + r, 16, stride=8), :
                    ]
    def pair_copy(i):
        tiles = pl.ds(i * 128, 128)
        return pltpu.make_async_remote_copy(
            q.at[1 - core, tiles], pair.at[tiles], pair_ss.at[i], pair_rs.at[i], device_id=mate, device_id_type=MESH
        )

    for i in range(4):
        pair_copy(i).start()
    for i in range(4):
        pair_copy(i).wait()
        tiles = pl.ds(i * 128, 128)
        h[pl.ds(i * 16, 16)] = (q[core, tiles] + pair[tiles]).reshape(16, 8, 128)

    @pl.loop(0, 64)
    def _(k):
        to = (k // 4 % 4, k % 4, k // 16)
        from_it = (x - to[0] + 4) % 4 * 16 + (y - to[1] + 4) % 4 * 4 + (z - to[2] + 4) % 4

        @pl.when(from_it != 0)
        def _():
            pltpu.make_async_remote_copy(
                h.at[to[0] * 16 + to[1] * 4 + to[2]], recv_h.at[from_it], all_sem.at[0], all_sem.at[1],
                device_id=ident(to, core), device_id_type=MESH,
            ).start()

    @pl.loop(0, ROWS // 4)
    def _(step):
        for j in range(4):
            i = step * 4 + j
            row = sums[table[0, i]]
            applied_out[0, i] = row[0:BS].astype(BF16)
            applied_out[1, i] = row[BS:2 * BS].astype(BF16)

    for d, (may_send, _, _) in enumerate(sides):
        @pl.when(may_send)
        def _():
            rows_copy(d, d).wait_send()
            for copy in half_copies(d, 0, d):
                copy.wait_send()

        special = s == by_corner[d][0] if d in by_corner else detours[d]

        @pl.when(jnp.logical_and(may_send, jnp.logical_not(special)))
        def _():
            for copy in half_copies(d, 1, d):
                copy.wait_send()

        if d not in by_corner:
            @pl.when(special)
            def _():
                for copy in half_copies(d, 1, d, HALF - DETOUR):
                    copy.wait_send()

    @pl.when(passes_on)
    def _():
        for k in range(DETOUR):
            for copy in side_onward_copies(k):
                copy.wait_send()

    for d, sender, corner, receiver in corners:
        @pl.when(s == sender)
        def _():
            for k in range(HALF):
                for copy in corner_copies(d, corner, k):
                    copy.wait_send()

        @pl.when(s == corner)
        def _():
            for k in range(HALF):
                for copy in onward_copies(receiver, k):
                    copy.wait_send()

    pltpu.make_async_remote_copy(
        h.at[pl.ds(1, 63)], recv_h.at[pl.ds(1, 63)], all_sem.at[0], all_sem.at[1], device_id=mate, device_id_type=MESH
    ).wait()
    recv_h[0] = h[x * 16 + y * 4 + z]


PIECES = 4


def write_out(applied, tiles, applied_out, reduced_out, reduced, sems, sem):
    copies = []
    for term in range(2):
        for piece in range(PIECES):
            rows = pl.ds(piece * (ROWS // PIECES), ROWS // PIECES)
            copies.append(pltpu.make_async_copy(applied.at[term, rows], applied_out.at[term, rows], sems.at[term, piece]))
    for copy in copies:
        copy.start()
    mine = tiles[...].reshape(8, 8, 8, 128).sum(axis=1).sum(axis=0)
    for r in range(2):
        for lanes in range(4):
            reduced[r, lanes // 2:lanes // 2 + 1, (lanes % 2) * 128:(lanes % 2 + 1) * 128] = mine[
                lanes * 2 + r:lanes * 2 + r + 1
            ]
    copies.append(pltpu.make_async_copy(reduced, reduced_out, sem))
    copies[-1].start()
    for copy in copies:
        copy.wait()


def local(basis, volume, own_blocks, own_cols, border_blocks, border_cols, border_rows):
    norm = 1.0 / math.sqrt(lax.axis_size("stream") * lax.axis_size("cross") * ROWS * BS)
    vmem = pl.BlockSpec(memory_space=pltpu.VMEM)
    anywhere = pl.BlockSpec(memory_space=pl.ANY)
    dma = pltpu.SemaphoreType.DMA
    applied, tiles = pl.pallas_call(
        functools.partial(kernel, norm),
        name="galerkin",
        in_specs=[anywhere] * 7,
        out_specs=[vmem, vmem],
        out_shape=[
            pltpu.VMEM((2, ROWS, BS, MODES), BF16),
            pltpu.VMEM((64, 8, 128), F32),
        ],
        scratch_shapes=[
            pltpu.SMEM((KOWN, ROWS), I32),
            pltpu.SMEM((4, NB), I32),
            pltpu.SMEM((4, NB), I32),
            pltpu.VMEM((ROWS // 2, 128), F32),
            pltpu.VMEM((ROWS, KOWN, BS, 2 * BS), BF16),
            pltpu.VMEM((ROWS, BS, MODES), BF16),
            pltpu.VMEM((ROWS + SLOTS, 2 * BS, MODES), F32),
            pltpu.VMEM((ROWS, BS, 128), F32),
            pltpu.VMEM((4, NB, 128), I32),
            pltpu.VMEM((4, NB, BS, MODES), BF16),
            pltpu.VMEM((4, NB, 128), I32),
            pltpu.VMEM((4, NB, BS, 2 * BS), BF16),
            pltpu.VMEM((4, NB, BS, MODES), BF16),
            pltpu.VMEM((HALF, BS, 2 * BS), BF16),
            pltpu.VMEM((HALF, BS, MODES), BF16),
            pltpu.VMEM((DETOUR, BS, 2 * BS), BF16),
            pltpu.VMEM((DETOUR, BS, MODES), BF16),
            pltpu.VMEM((8, 128), I32),
            pltpu.SMEM((8, 128), I32),
            pltpu.VMEM((PROJ, BS, 2 * MODES), BF16),
            pltpu.VMEM((NB, BS, 2 * MODES), BF16),
            pltpu.VMEM((4, MODES, 128), F32),
            pltpu.VMEM((2, 512, 128), F32),
            pltpu.VMEM((512, 128), F32),
            pltpu.VMEM((64, 8, 128), F32),
            dma((STEPS,)), dma(()), dma((4,)), dma(()),
            dma((4,)), dma((4,)), dma((4, 2)), dma((4, 2)), dma((4, 2)), dma((4, 2)),
            dma((2, HALF)), dma((2, HALF)), dma((2, HALF)),
            dma((2, DETOUR)), dma((2, DETOUR)), dma((2, DETOUR)),
            dma((4,)), dma((4,)), dma((2,)), pltpu.SemaphoreType.REGULAR((len(ROUNDS),)),
        ],
        compiler_params=pltpu.CompilerParams(
            collective_id=0, has_side_effects=True, vmem_limit_bytes=48 << 20
        ),
        cost_estimate=pl.CostEstimate(flops=4_700_000_000, bytes_accessed=21_000_000, transcendentals=0),
    )(
        own_cols.T,
        border_cols[0],
        border_rows[0],
        basis.reshape(ROWS, BS, MODES),
        volume.reshape(ROWS // 2, 128),
        own_blocks,
        border_blocks[0],
    )
    applied, reduced = pl.pallas_call(
        write_out,
        name="write_out",
        in_specs=[pl.BlockSpec(memory_space=pltpu.VMEM)] * 2,
        out_specs=[anywhere, anywhere],
        out_shape=[
            jax.ShapeDtypeStruct((2, ROWS, BS, MODES), BF16),
            jax.ShapeDtypeStruct((2, 2, MODES), F32),
        ],
        scratch_shapes=[pltpu.VMEM((2, 2, MODES), F32), dma((2, PIECES)), dma(())],
        compiler_params=pltpu.CompilerParams(vmem_limit_bytes=16 << 20),
    )(applied, tiles)
    applied = applied.reshape(2, ROWS * BS, MODES)
    return applied, reduced


def solution(mesh):
    both = ("stream", "cross")
    return jax.shard_map(
        local,
        mesh=mesh,
        in_specs=(
            P(both, None), P(both), P(both, None, None, None), P(both, None),
            P(both, None, None, None, None), P(both, None, None), P(both, None, None),
        ),
        out_specs=(P(None, both, None), P(both, None, None)),
        check_vma=False,
    )
```
